256 devices in a mesh: section: 8 (over z), dp: 32 (over y, x, core).
Axes of the slice: x: 4, y: 4, z: 8, core: 2. Of those that a mesh axis runs over, the one named last changes fastest.
Arguments:
- acts: bfloat16 [8, 4096, 2560], P('section', 'dp'), may hold values from -48 to 48
- out_grad: bfloat16 [4096, 2560], P('dp'), may hold values from -6 to 6
- tok_count: int32 [32], P('dp'), may hold values from 42 to 128, as said below
- norm_gain: float32 [8, 2560], P('section'), may hold values from 0.25 to 1.75
- w_value: bfloat16 [8, 2560, 512], P('section'), may hold values from -0.125 to 0.125
- w_out: bfloat16 [8, 512, 2560], P('section'), may hold values from -0.25 to 0.25
- err_value: bfloat16 [8, 81920, 512], P('section', 'dp'), may hold values from -0.59765625 to 0.59765625
- err_out: bfloat16 [8, 16384, 2560], P('section', 'dp'), may hold values from -0.59765625 to 0.59765625
- start_q_value: float32 [8, 512, 8], P('section'), may hold values from -5 to 5
- start_q_out: float32 [8, 2560, 8], P('section'), may hold values from -5 to 5
Outputs:
- q_value: float32 [8, 512, 8], P('section')
- q_out: float32 [8, 2560, 8], P('section')
The draws below stay inside these ranges and needn't reach their ends.
Inputs may be any that keep to these rules, and one draw needn't show every extreme that they name: `tok_count`: in every draw one replica has all 128 slots counting and another exactly 42.
All inputs are finite; a program needn't handle non-finite values.
Results may differ from the reference program's by a relative error of at most 0.03.
Values may be sent and summed in bfloat16 or wider, within the bound.
A program may use at most 64 MiB of HBM per device.

```python
import math
import jax
import jax.numpy as jnp
from jax import lax

DW = 2560
HV = 512
RANK = 8
ROWS = 128
SECTIONS = 8
REPLICAS = 32
TOKENS = 4096
N_DP = 32


def draw_acts(key, part):
    key = jax.random.fold_in(key, 11)
    k_base, k_row, k_col = jax.random.split(key, 3)
    full_shape = (SECTIONS, TOKENS, DW)
    base_draw = jnp.clip(jax.random.normal(k_base, full_shape, jnp.float32), -4.0, 4.0)
    row_scale = jnp.exp(jax.random.uniform(k_row, (SECTIONS, TOKENS, 1), jnp.float32, math.log(0.3), math.log(3.0)))
    col_scale = jnp.exp(jax.random.uniform(k_col, (SECTIONS, 1, DW), jnp.float32, math.log(0.4), math.log(4.0)))
    return (base_draw * row_scale * col_scale).astype(jnp.bfloat16)


def draw_tok_count(key, part):
    key = jax.random.fold_in(key, 12)
    k_all, k_top, k_low = jax.random.split(key, 3)
    counts = jax.random.randint(k_all, (REPLICAS,), ROWS // 3, ROWS + 1)
    top_index = jax.random.randint(k_top, (), 0, REPLICAS)
    low_index = (top_index + jax.random.randint(k_low, (), 1, REPLICAS)) % REPLICAS
    replica_ids = jnp.arange(REPLICAS)
    counts = jnp.where(replica_ids == top_index, ROWS, counts)
    counts = jnp.where(replica_ids == low_index, ROWS // 3, counts)
    return counts.astype(jnp.int32)


def steps_of(key, extent, cuts, smallest, largest):
    def one(dim, shards_of):
        draws = jax.random.uniform(jax.random.fold_in(jax.random.fold_in(key, 6), dim), (shards_of,), jnp.float32, smallest / len(cuts), largest / len(cuts))
        return jnp.repeat(jnp.exp(draws), extent[dim] // shards_of).reshape((-1,) + (1,) * (len(extent) - dim - 1))

    factor_of = one(*cuts[0])
    for cut in cuts[1:]:
        factor_of = factor_of * one(*cut)
    return factor_of


def scatter_about(own_key, dims, deviation, most, cuts=(), dtype=jnp.bfloat16):
    values = deviation * jax.random.normal(own_key, dims, jnp.float32)
    if cuts:
        values = values * steps_of(own_key, dims, cuts, -0.22, 0.18)
    return jnp.clip(values, -most, most).astype(dtype)


def setup_inputs(seed: int = 0) -> dict:
    key_list = jax.random.split(jax.random.key(seed), 11)
    acts = draw_acts(jax.random.fold_in(key_list[10], 71), 0)
    out_grad = scatter_about(key_list[1], (TOKENS, DW), 1.0, 6.0, ((0, 32),))
    tok_count = draw_tok_count(jax.random.fold_in(key_list[10], 71), 0)
    norm_gain = jnp.clip(1.0 + 0.15 * jax.random.normal(key_list[3], (SECTIONS, DW), jnp.float32), 0.25, 1.75)
    w_value = scatter_about(key_list[4], (SECTIONS, DW, HV), DW ** -0.5, 0.125, ((0, 8),))
    w_out = scatter_about(key_list[5], (SECTIONS, HV, DW), HV ** -0.5, 0.25, ((0, 8),))
    err_value = scatter_about(key_list[6], (SECTIONS, REPLICAS * DW, HV), 0.1, 0.59765625, ((0, 8), (1, 32)))
    err_out = scatter_about(key_list[7], (SECTIONS, REPLICAS * HV, DW), 0.1, 0.59765625, ((0, 8), (1, 32)))
    start_q_value = scatter_about(key_list[8], (SECTIONS, HV, RANK), 1.0, 5.0, ((0, 8),), jnp.float32)
    start_q_out = scatter_about(key_list[9], (SECTIONS, DW, RANK), 1.0, 5.0, ((0, 8),), jnp.float32)
    return dict(acts=acts, out_grad=out_grad, tok_count=tok_count, norm_gain=norm_gain, w_value=w_value, w_out=w_out, err_value=err_value, err_out=err_out, start_q_value=start_q_value, start_q_out=start_q_out)


epsilon = 1e-06
highest = lax.Precision.HIGHEST

def rms_parts(rows_in):
    widened = rows_in.astype(jnp.float32)
    inv_rms = lax.rsqrt(lax.optimization_barrier(jnp.mean(widened * widened, axis=-1, keepdims=True)) + epsilon)
    return (inv_rms, widened * inv_rms)

def orthonormal(basis_raw):
    gram_matrix = jnp.dot(basis_raw.T.astype(jnp.float32), basis_raw.astype(jnp.float32), precision=highest, preferred_element_type=jnp.float32)
    lower_factor = jnp.linalg.cholesky(gram_matrix)
    return jax.scipy.linalg.solve_triangular(lower_factor, basis_raw.T, lower=True).T

def reference(acts, out_grad, tok_count, norm_gain, w_value, w_out, err_value, err_out, start_q_value, start_q_out):
    scale_down = tok_count.astype(jnp.float32)[:, None, None]
    live_mask = (jnp.arange(ROWS)[None, :] < tok_count[:, None]).reshape(TOKENS, 1)
    grad_now = jnp.where(live_mask, out_grad, jnp.zeros_like(out_grad))
    section_grads = [grad_now for section in range(SECTIONS)]
    for section in range(SECTIONS - 1, 0, -1):
        section_grads[section] = grad_now
        inv_rms, unit_rows = rms_parts(acts[section])
        value_grad = jnp.dot(grad_now.astype(jnp.float32), w_out[section].T.astype(jnp.float32), preferred_element_type=jnp.float32).astype(jnp.bfloat16)
        norm_grad = jnp.dot(value_grad.astype(jnp.float32), w_value[section].T.astype(jnp.float32), preferred_element_type=jnp.float32)
        scaled = norm_grad * norm_gain[section]
        centred = scaled - unit_rows * lax.optimization_barrier(jnp.mean(scaled * unit_rows, axis=-1, keepdims=True))
        grad_now = (grad_now.astype(jnp.float32) + inv_rms * centred).astype(jnp.bfloat16)
    section_grads[0] = grad_now
    q_values = []
    q_outs = []
    for section in range(SECTIONS):
        inv_rms, unit_rows = rms_parts(acts[section])
        normed = (unit_rows * norm_gain[section]).astype(jnp.bfloat16)
        grad_here = section_grads[section]
        value_grad = jnp.dot(grad_here.astype(jnp.float32), w_out[section].T.astype(jnp.float32), preferred_element_type=jnp.float32).astype(jnp.bfloat16)
        values = jnp.dot(normed.astype(jnp.float32), w_value[section].astype(jnp.float32), preferred_element_type=jnp.float32).astype(jnp.bfloat16)
        normed_split = normed.reshape(N_DP, ROWS, DW).astype(jnp.float32)
        vgrad_split = value_grad.reshape(N_DP, ROWS, HV).astype(jnp.float32)
        values_split = values.reshape(N_DP, ROWS, HV).astype(jnp.float32)
        grad_split = grad_here.reshape(N_DP, ROWS, DW).astype(jnp.float32)
        m_value = jnp.einsum('xtd,xth->xdh', normed_split, vgrad_split) / scale_down
        m_value = m_value + err_value[section].reshape(N_DP, DW, HV).astype(jnp.float32)
        m_out = jnp.einsum('xth,xtd->xhd', values_split, grad_split) / scale_down
        m_out = m_out + err_out[section].reshape(N_DP, HV, DW).astype(jnp.float32)
        p_value = jnp.einsum('xdh,hk->dk', m_value, start_q_value[section], precision=highest)
        p_out = jnp.einsum('xhd,dk->hk', m_out, start_q_out[section], precision=highest)
        basis_value = orthonormal(p_value)
        basis_out = orthonormal(p_out)
        q_values.append(jnp.einsum('xdh,dk->hk', m_value, basis_value, precision=highest))
        q_outs.append(jnp.einsum('xhd,hk->dk', m_out, basis_out, precision=highest))
    return (jnp.stack(q_values), jnp.stack(q_outs))
```

```python
import functools

import jax
import jax.numpy as jnp
from jax import lax
from jax.experimental import pallas as pl
from jax.experimental.pallas import tpu as pltpu
from jax.sharding import PartitionSpec as P

EPSILON = 1e-06
LANES = 128
BF16 = jnp.bfloat16
F32 = jnp.float32


def mm(a, b):
    return lax.dot_general(a, b, (((1,), (0,)), ((), ())), preferred_element_type=F32)


def mm_nt(a, b):
    return lax.dot_general(a, b, (((1,), (1,)), ((), ())), preferred_element_type=F32)


def split(x):
    high = x.astype(BF16).astype(F32)
    return jnp.concatenate([high, x - high], axis=0).astype(BF16)


def joined(product):
    half = product.shape[0] // 2
    return product[:half] + product[half:]


def small_mm(x, big):
    return joined(mm(split(x), big))


def small_mm_nt(x, big):
    return joined(mm_nt(split(x), big))


def inverse_factor(gram):
    n = gram.shape[0]
    row = lax.broadcasted_iota(jnp.int32, (n, n), 0)
    col = lax.broadcasted_iota(jnp.int32, (n, n), 1)
    work = jnp.concatenate([gram, jnp.where(row == col, 1.0, 0.0)], axis=1)
    line = lax.broadcasted_iota(jnp.int32, (n, 2 * n), 0)
    for k in range(n):
        root = lax.rsqrt(work[k : k + 1, k : k + 1])
        pivot = work[k : k + 1, :] * root
        factor = work[:, k : k + 1] * root
        work = jnp.where(line == k, pivot, jnp.where(line > k, work - factor * pivot, work))
    return work[:, n:]


def apply_small(lower, tile):
    total = lower[:, 0:1] * tile[0:1, :]
    for k in range(1, lower.shape[1]):
        total = total + lower[:, k : k + 1] * tile[k : k + 1, :]
    return total


def kernel(
    sections,
    replicas,
    blocks,
    acts_hbm,
    top_hbm,
    count_ref,
    gain_hbm,
    w_value_hbm,
    w_out_hbm,
    err_value_hbm,
    err_out_hbm,
    q_value_hbm,
    q_out_hbm,
    out_value,
    out_out,
    acts,
    top,
    gain,
    w_value,
    w_out,
    err_value,
    err_out,
    start_value,
    start_out,
    w_value_t,
    w_out_t,
    unit,
    inv_rms,
    normed,
    values,
    grads,
    passed,
    value_grad,
    norm_grad,
    p_part,
    p_all,
    q_part,
    q_all,
    p_seen,
    q_seen,
    load_sem,
    relay_send,
    relay_recv,
    reduce_send,
    reduce_recv,
):
    section = lax.axis_index("section")
    me = lax.axis_index("dp")
    rows, dw = acts.shape
    hv = w_out.shape[0]
    size = rows // blocks
    value_tiles, out_tiles = dw // LANES, hv // LANES
    tiles = value_tiles + out_tiles
    last = sections - 1

    loads = [
        pltpu.make_async_copy(src, dst, load_sem.at[i])
        for i, (src, dst) in enumerate(
            [
                (w_out_hbm, w_out),
                (top_hbm, top),
                (acts_hbm, acts),
                (gain_hbm, gain),
                (w_value_hbm, w_value),
                (q_value_hbm, start_value),
                (q_out_hbm, start_out),
                (err_value_hbm, err_value),
                (err_out_hbm, err_out),
            ]
        )
    ]
    for load in loads:
        load.start()
    (l_w_out, l_top, l_acts, l_gain, l_w_value, l_q_value, l_q_out, l_err_value, l_err_out) = loads

    barrier = pltpu.get_barrier_semaphore()

    def greet(k, carry):
        pl.semaphore_signal(
            barrier, inc=1, device_id={"dp": lax.rem(me + k, replicas)}, device_id_type=pl.DeviceIdType.MESH
        )
        return carry

    for step in (1, sections - 1):
        pl.semaphore_signal(
            barrier,
            inc=1,
            device_id={"section": lax.rem(section + step, sections)},
            device_id_type=pl.DeviceIdType.MESH,
        )
    lax.fori_loop(1, replicas, greet, 0)

    count = count_ref[0]
    scale = 1.0 / jnp.full((1, 1), count, jnp.int32).astype(F32)

    def block_rows(b):
        return pl.ds(pl.multiple_of(b * size, size), size)

    def normalise():
        def body(b, carry):
            here = block_rows(b)
            wide = acts[here, :].astype(F32)
            inv = lax.rsqrt(jnp.mean(wide * wide, axis=-1, keepdims=True) + EPSILON)
            unit_rows = wide * inv
            inv_rms[here, :] = jnp.broadcast_to(inv, (size, LANES))
            unit[here, :] = unit_rows
            normed[here, :] = (unit_rows * gain[...]).astype(BF16)
            return carry

        lax.fori_loop(0, blocks, body, 0)

    def error_parts():
        p_part[:, :dw] = small_mm_nt(start_value[...], err_value[...])
        p_part[:, dw:] = small_mm_nt(start_out[...], err_out[...])

    def hop(b):
        here = block_rows(b)
        return pltpu.make_async_remote_copy(
            src_ref=passed.at[here],
            dst_ref=grads.at[here],
            send_sem=relay_send.at[b],
            recv_sem=relay_recv.at[b],
            device_id={"section": lax.rem(section + last, sections)},
            device_id_type=pl.DeviceIdType.MESH,
        )

    def pass_on(b, product):
        here = block_rows(b)
        scaled = product * gain[...]
        unit_rows = unit[here, :]
        centred = scaled - unit_rows * jnp.mean(scaled * unit_rows, axis=-1, keepdims=True)
        inv = inv_rms[here, 0:1]
        passed[here, :] = (grads[here, :].astype(F32) + inv * centred).astype(BF16)
        hop(b).start()

    @pl.when(section == last)
    def _():
        l_top.wait()
        live = lax.broadcasted_iota(jnp.int32, (rows, 1), 0) < count
        grads[...] = jnp.where(live, top[...].astype(F32), 0.0).astype(BF16)
        l_w_out.wait()
        value_grad[...] = mm_nt(grads[...], w_out[...]).astype(BF16)
        l_acts.wait()
        l_gain.wait()
        normalise()
        l_w_value.wait()
        norm_grad[...] = mm_nt(value_grad[...], w_value[...])
        pl.semaphore_wait(barrier, replicas + 1)

        def body(b, carry):
            pass_on(b, norm_grad[block_rows(b), :])
            return carry

        lax.fori_loop(0, blocks, body, 0)
        values[...] = mm(normed[...], w_value[...]).astype(BF16)
        for load in (l_q_value, l_q_out, l_err_value, l_err_out):
            load.wait()
        error_parts()

    @pl.when(section < last)
    def _():
        l_w_out.wait()
        w_out_t[...] = w_out[...].T
        l_acts.wait()
        l_gain.wait()
        normalise()
        l_w_value.wait()
        w_value_t[...] = w_value[...].T
        values[...] = mm(normed[...], w_value[...]).astype(BF16)
        for load in (l_top, l_q_value, l_q_out, l_err_value, l_err_out):
            load.wait()
        error_parts()
        pl.semaphore_wait(barrier, replicas + 1)

        def body(b, carry):
            here = block_rows(b)
            hop(b).wait_recv()
            v_rows = mm(grads[here, :], w_out_t[...]).astype(BF16)
            value_grad[here, :] = v_rows

            @pl.when(section > 0)
            def _():
                pass_on(b, mm(v_rows, w_value_t[...]))

            return carry

        lax.fori_loop(0, blocks, body, 0)

    def exchange(part, seen, total, phase, finish):
        def tile(ref, j):
            return ref.at[:, pl.ds(pl.multiple_of(j * LANES, LANES), LANES)]

        def scatter(k, carry):
            owner = lax.rem(me + k, replicas)

            @pl.when(owner < tiles)
            def _():
                pltpu.make_async_remote_copy(
                    src_ref=tile(part, owner),
                    dst_ref=seen.at[me],
                    send_sem=reduce_send.at[2 * phase],
                    recv_sem=reduce_recv.at[2 * phase],
                    device_id={"dp": owner},
                    device_id_type=pl.DeviceIdType.MESH,
                ).start()

            return carry

        lax.fori_loop(1, replicas, scatter, 0)
        extra = finish[0]()

        def arrivals(sem, amount):
            return pltpu.make_async_copy(seen.at[pl.ds(0, amount)], seen.at[pl.ds(0, amount)], sem)

        def spread(k):
            return pltpu.make_async_remote_copy(
                src_ref=tile(total, me),
                dst_ref=tile(total, me),
                send_sem=reduce_send.at[2 * phase + 1],
                recv_sem=reduce_recv.at[2 * phase + 1],
                device_id={"dp": lax.rem(me + k, replicas)},
                device_id_type=pl.DeviceIdType.MESH,
            )

        @pl.when(me < tiles)
        def _():
            seen[me] = tile(part, me)[...]
            arrivals(reduce_recv.at[2 * phase], replicas - 1).wait()
            tile(total, me)[...] = finish[1](jnp.sum(seen[...], axis=0), extra)

            def body(k, carry):
                spread(k).start()
                return carry

            lax.fori_loop(1, replicas, body, 0)
            arrivals(reduce_recv.at[2 * phase + 1], tiles - 1).wait()
            arrivals(reduce_send.at[2 * phase], tiles - 1).wait()
            arrivals(reduce_send.at[2 * phase + 1], replicas - 1).wait()

        @pl.when(me >= tiles)
        def _():
            arrivals(reduce_recv.at[2 * phase + 1], tiles).wait()
            arrivals(reduce_send.at[2 * phase], tiles).wait()

    p_part[:, :dw] += small_mm(small_mm_nt(start_value[...], value_grad[...]) * scale, normed[...])
    p_part[:, dw:] += small_mm(small_mm_nt(start_out[...], grads[...]) * scale, values[...])
    exchange(p_part, p_seen, p_all, 0, (lambda: None, lambda tile, extra: tile))

    p_value, p_out = p_all[:, :dw], p_all[:, dw:]
    q_part[:, :hv] = small_mm(small_mm_nt(p_value, normed[...]) * scale, value_grad[...]) + small_mm(
        p_value, err_value[...]
    )
    q_part[:, hv:] = small_mm(small_mm_nt(p_out, values[...]) * scale, grads[...]) + small_mm(
        p_out, err_out[...]
    )

    def factors():
        grams = [
            lax.dot_general(
                x, x, (((1,), (1,)), ((), ())), precision=lax.Precision.HIGHEST, preferred_element_type=F32
            )
            for x in (p_all[:, :dw], p_all[:, dw:])
        ]
        return [inverse_factor(gram) for gram in grams]

    def solved(tile, extra):
        for_value, for_out = extra
        return apply_small(jnp.where(me < out_tiles, for_value, for_out), tile)

    exchange(q_part, q_seen, q_all, 1, (factors, solved))
    out_value[...] = q_all[:, :hv]
    out_out[...] = q_all[:, hv:]

    @pl.when(section > 0)
    def _():
        def body(b, carry):
            hop(b).wait_send()
            return carry

        lax.fori_loop(0, blocks, body, 0)


def solution(mesh):
    sections, replicas = mesh.shape["section"], mesh.shape["dp"]

    def shards(
        acts, out_grad, tok_count, norm_gain, w_value, w_out, err_value, err_out, start_q_value, start_q_out
    ):
        rows, dw = out_grad.shape
        hv, rank = start_q_value.shape[1:]
        blocks = rows // 16
        any_space = pl.BlockSpec(memory_space=pl.ANY)
        vmem = pl.BlockSpec(memory_space=pltpu.VMEM)
        q_value, q_out = pl.pallas_call(
            functools.partial(kernel, sections, replicas, blocks),
            out_shape=(
                jax.ShapeDtypeStruct((rank, hv), F32),
                jax.ShapeDtypeStruct((rank, dw), F32),
            ),
            in_specs=[any_space] * 2 + [pl.BlockSpec(memory_space=pltpu.SMEM)] + [any_space] * 7,
            out_specs=(vmem, vmem),
            scratch_shapes=[
                pltpu.VMEM((rows, dw), BF16),
                pltpu.VMEM((rows, dw), BF16),
                pltpu.VMEM((1, dw), F32),
                pltpu.VMEM((dw, hv), BF16),
                pltpu.VMEM((hv, dw), BF16),
                pltpu.VMEM((dw, hv), BF16),
                pltpu.VMEM((hv, dw), BF16),
                pltpu.VMEM((rank, hv), F32),
                pltpu.VMEM((rank, dw), F32),
                pltpu.VMEM((hv, dw), BF16),
                pltpu.VMEM((dw, hv), BF16),
                pltpu.VMEM((rows, dw), F32),
                pltpu.VMEM((rows, LANES), F32),
                pltpu.VMEM((rows, dw), BF16),
                pltpu.VMEM((rows, hv), BF16),
                pltpu.VMEM((rows, dw), BF16),
                pltpu.VMEM((rows, dw), BF16),
                pltpu.VMEM((rows, hv), BF16),
                pltpu.VMEM((rows, dw), F32),
                pltpu.VMEM((rank, dw + hv), F32),
                pltpu.VMEM((rank, dw + hv), F32),
                pltpu.VMEM((rank, dw + hv), F32),
                pltpu.VMEM((rank, dw + hv), F32),
                pltpu.VMEM((replicas, rank, LANES), F32),
                pltpu.VMEM((replicas, rank, LANES), F32),
                pltpu.SemaphoreType.DMA((9,)),
                pltpu.SemaphoreType.DMA((blocks,)),
                pltpu.SemaphoreType.DMA((blocks,)),
                pltpu.SemaphoreType.DMA((4,)),
                pltpu.SemaphoreType.DMA((4,)),
            ],
            compiler_params=pltpu.CompilerParams(
                collective_id=0, has_side_effects=True, vmem_limit_bytes=48 * 2**20
            ),
            cost_estimate=pl.CostEstimate(flops=1_700_000_000, bytes_accessed=12_000_000, transcendentals=0),
        )(
            acts[0],
            out_grad,
            tok_count,
            norm_gain,
            w_value[0],
            w_out[0],
            err_value[0],
            err_out[0],
            start_q_value[0].T,
            start_q_out[0].T,
        )
        return q_value.T[None], q_out.T[None]

    placed = (
        P("section", "dp", None),
        P("dp", None),
        P("dp"),
        P("section", None),
        P("section", None, None),
        P("section", None, None),
        P("section", "dp", None),
        P("section", "dp", None),
        P("section", None, None),
        P("section", None, None),
    )
    return jax.shard_map(
        shards,
        mesh=mesh,
        in_specs=placed,
        out_specs=(P("section", None, None), P("section", None, None)),
        check_vma=False,
    )
```

```python
import functools

import jax
import jax.numpy as jnp
from jax import lax
from jax.experimental import pallas as pl
from jax.experimental.pallas import tpu as pltpu
from jax.sharding import PartitionSpec as P

EPSILON = 1e-06
LANES = 128
CUTS = (0, 5, 10, 15, 20)
GROUPS = ((0,), (1,), (2,), (3,))
BF16 = jnp.bfloat16
F32 = jnp.float32


def mm(a, b):
    return lax.dot_general(a, b, (((1,), (0,)), ((), ())), preferred_element_type=F32)


def mm_nt(a, b):
    return lax.dot_general(a, b, (((1,), (1,)), ((), ())), preferred_element_type=F32)


def split(x):
    high = x.astype(BF16).astype(F32)
    return jnp.concatenate([high, x - high], axis=0).astype(BF16)


def joined(product):
    half = product.shape[0] // 2
    return product[:half] + product[half:]


def small_mm(x, big):
    return joined(mm(split(x), big))


def small_mm_nt(x, big):
    return joined(mm_nt(split(x), big))


def inverse_factor(gram):
    n = gram.shape[0]
    row = lax.broadcasted_iota(jnp.int32, (n, n), 0)
    col = lax.broadcasted_iota(jnp.int32, (n, n), 1)
    work = jnp.concatenate([gram, jnp.where(row == col, 1.0, 0.0)], axis=1)
    line = lax.broadcasted_iota(jnp.int32, (n, 2 * n), 0)
    for k in range(n):
        root = lax.rsqrt(work[k : k + 1, k : k + 1])
        pivot = work[k : k + 1, :] * root
        factor = work[:, k : k + 1] * root
        work = jnp.where(line == k, pivot, jnp.where(line > k, work - factor * pivot, work))
    return work[:, n:]


def apply_small(lower, tile):
    total = lower[:, 0:1] * tile[0:1, :]
    for k in range(1, lower.shape[1]):
        total = total + lower[:, k : k + 1] * tile[k : k + 1, :]
    return total


def kernel(
    sections,
    replicas,
    blocks,
    cuts,
    groups,
    acts_hbm,
    top_hbm,
    count_ref,
    gain_hbm,
    w_value_hbm,
    w_out_hbm,
    err_value_hbm,
    err_out_hbm,
    q_value_hbm,
    q_out_hbm,
    out_ref,
    acts,
    top,
    gain,
    w_value,
    w_out,
    err_value,
    err_out,
    start_value,
    start_out,
    w_value_t,
    w_out_t,
    unit,
    inv_rms,
    normed,
    values,
    values_wide,
    grads,
    passed,
    value_grad,
    norm_grad,
    p_part,
    p_all,
    p_packed,
    q_packed,
    p_total,
    q_total,
    p_seen,
    q_seen,
    load_sem,
    relay_send,
    relay_recv,
    reduce_send,
    reduce_recv,
):
    section = lax.axis_index("section")
    me = lax.axis_index("dp")
    rows, dw = acts.shape
    hv = w_out.shape[0]
    size = rows // blocks
    value_tiles, out_tiles = dw // (2 * LANES), hv // (2 * LANES)
    tiles = value_tiles + out_tiles
    last = sections - 1
    chips = replicas // 2
    chip, core = me // 2, lax.rem(me, 2)
    owner = (core == 1) & (chip < tiles)
    pieces = len(cuts) - 1

    loads = [
        pltpu.make_async_copy(src, dst, load_sem.at[i])
        for i, (src, dst) in enumerate(
            [
                (top_hbm, top),
                (w_out_hbm, w_out),
                (acts_hbm, acts),
                (gain_hbm, gain),
                (w_value_hbm, w_value),
                (q_value_hbm, start_value),
                (q_out_hbm, start_out),
                (err_value_hbm, err_value),
                (err_out_hbm, err_out),
            ]
        )
    ]
    (l_top, l_w_out, l_acts, l_gain, l_w_value, l_q_value, l_q_out, l_err_value, l_err_out) = loads
    for load in loads[:4]:
        load.start()

    barrier = pltpu.get_barrier_semaphore()

    def greet(k, carry):
        pl.semaphore_signal(
            barrier, inc=1, device_id={"dp": lax.rem(me + k, replicas)}, device_id_type=pl.DeviceIdType.MESH
        )
        return carry

    for step in (1, sections - 1):
        pl.semaphore_signal(
            barrier,
            inc=1,
            device_id={"section": lax.rem(section + step, sections)},
            device_id_type=pl.DeviceIdType.MESH,
        )
    lax.fori_loop(1, replicas, greet, 0)

    count = count_ref[0]
    scale = 1.0 / jnp.full((1, 1), count, jnp.int32).astype(F32)

    def block_rows(b):
        return pl.ds(pl.multiple_of(b * size, size), size)

    def normalise(b):
        here = block_rows(b)
        wide = acts[here, :].astype(F32)
        inv = lax.rsqrt(jnp.mean(wide * wide, axis=-1, keepdims=True) + EPSILON)
        unit_rows = wide * inv
        inv_rms[here, :] = jnp.broadcast_to(inv, (size, LANES))
        unit[here, :] = unit_rows
        normed[here, :] = (unit_rows * gain[...]).astype(BF16)

    def each_block(work):
        def body(b, carry):
            work(b)
            return carry

        lax.fori_loop(0, blocks, body, 0)

    def error_parts():
        p_part[:, :dw] = small_mm_nt(start_value[...], err_value[...])
        p_part[:, dw:] = small_mm_nt(start_out[...], err_out[...])

    def add_block(here):
        p_part[:, :dw] += small_mm(small_mm_nt(start_value[...], value_grad[here, :]) * scale, normed[here, :])
        p_part[:, dw:] += small_mm(small_mm_nt(start_out[...], grads[here, :]) * scale, values[here, :])

    def piece(c):
        return slice(cuts[c], cuts[c + 1])

    def hop(b, c):
        return pltpu.make_async_remote_copy(
            src_ref=passed.at[block_rows(b), piece(c)],
            dst_ref=grads.at[block_rows(b), piece(c)],
            send_sem=relay_send.at[b * pieces + c],
            recv_sem=relay_recv.at[b * pieces + c],
            device_id={"section": lax.rem(section + last, sections)},
            device_id_type=pl.DeviceIdType.MESH,
        )

    def pass_on(b, mean, product):
        here = block_rows(b)
        inv = inv_rms[here, 0:1]
        for c in range(pieces):
            cols = piece(c)
            centred = product(cols) * gain[:, cols] - unit[here, cols] * mean
            passed[here, cols] = (grads[here, cols].astype(F32) + inv * centred).astype(BF16)
            if c + 1 == 2:
                for early in range(2):
                    hop(b, early).start()
        for c in range(2, pieces):
            hop(b, c).start()

    def project():
        wide = mm(normed[...], w_value[...])
        values_wide[...] = wide
        values[...] = wide.astype(BF16)

    @pl.when(section == last)
    def _():
        l_top.wait()
        l_w_value.start()
        live = lax.broadcasted_iota(jnp.int32, (rows, 1), 0) < count
        grads[...] = jnp.where(live, top[...].astype(F32), 0.0).astype(BF16)
        l_w_out.wait()
        value_grad[...] = mm_nt(grads[...], w_out[...]).astype(BF16)
        l_acts.wait()
        l_gain.wait()
        l_w_value.wait()
        for load in loads[5:]:
            load.start()
        norm_grad[...] = mm_nt(value_grad[...], w_value[...])
        pl.semaphore_wait(barrier, replicas + 1)

        def send(b):
            here = block_rows(b)
            normalise(b)
            mean = jnp.mean(norm_grad[here, :] * gain[...] * unit[here, :], axis=-1, keepdims=True)
            pass_on(b, mean, lambda cols: norm_grad[here, cols])

        each_block(send)
        project()
        for load in loads[5:]:
            load.wait()
        error_parts()

    @pl.when(section < last)
    def _():
        l_acts.wait()
        l_w_value.start()
        l_gain.wait()
        for load in loads[5:]:
            load.start()
        each_block(normalise)
        l_w_out.wait()
        w_out_t[...] = w_out[...].T
        l_w_value.wait()
        w_value_t[...] = w_value[...].T
        project()
        for load in (l_top, *loads[5:]):
            load.wait()
        error_parts()
        pl.semaphore_wait(barrier, replicas + 1)

        def relay(b):
            here = block_rows(b)
            total = None
            for group in groups:
                for c in group:
                    hop(b, c).wait_recv()
                cols = slice(cuts[group[0]], cuts[group[-1] + 1])
                term = mm(grads[here, cols], w_out_t[cols, :])
                total = term if total is None else total + term
            v_rows = total.astype(BF16)
            value_grad[here, :] = v_rows

            @pl.when(section > 0)
            def _():
                mean = jnp.sum(v_rows.astype(F32) * values_wide[here, :], axis=-1, keepdims=True) * (1.0 / dw)
                pass_on(b, mean, lambda cols: mm(v_rows, w_value_t[:, cols]))

            @pl.when(section == 0)
            def _():
                add_block(here)

        each_block(relay)

    def packed(x):
        return jnp.concatenate([x[:, :LANES], x[:, LANES:]], axis=0).astype(BF16)

    def arrivals(ref, amount, sem):
        return pltpu.make_async_copy(ref.at[pl.ds(0, amount)], ref.at[pl.ds(0, amount)], sem)

    def far_first(k):
        return lax.rem(chip + chips // 2 + 2 + k, chips)

    def exchange(part, seen, total, phase, meanwhile, finish):
        def scatter(k, carry):
            to = far_first(k)

            @pl.when((to < tiles) & ((to != chip) | (core == 0)))
            def _():
                pltpu.make_async_remote_copy(
                    src_ref=part.at[to],
                    dst_ref=seen.at[me],
                    send_sem=reduce_send.at[2 * phase],
                    recv_sem=reduce_recv.at[2 * phase],
                    device_id={"dp": 2 * to + 1},
                    device_id_type=pl.DeviceIdType.MESH,
                ).start()

            return carry

        lax.fori_loop(0, chips, scatter, 0)
        extra = meanwhile()

        @pl.when(owner)
        def _():
            seen[me] = part[chip]
            arrivals(seen, replicas - 1, reduce_recv.at[2 * phase]).wait()
            total[chip] = finish(jnp.sum(seen[...].astype(F32), axis=0), extra).astype(BF16)

            def spread(k, carry):
                to = far_first(k)
                for end in range(2):

                    @pl.when((to != chip) | (end == 0))
                    def _():
                        pltpu.make_async_remote_copy(
                            src_ref=total.at[chip],
                            dst_ref=total.at[chip],
                            send_sem=reduce_send.at[2 * phase + 1],
                            recv_sem=reduce_recv.at[2 * phase + 1],
                            device_id={"dp": 2 * to + end},
                            device_id_type=pl.DeviceIdType.MESH,
                        ).start()

                return carry

            lax.fori_loop(0, chips, spread, 0)
            arrivals(total, tiles - 1, reduce_recv.at[2 * phase + 1]).wait()

        @pl.when(jnp.logical_not(owner))
        def _():
            arrivals(total, tiles, reduce_recv.at[2 * phase + 1]).wait()

    def finish_sends(seen, phase):
        @pl.when(owner)
        def _():
            arrivals(seen, tiles - 1, reduce_send.at[2 * phase]).wait()
            arrivals(seen, replicas - 1, reduce_send.at[2 * phase + 1]).wait()

        @pl.when(jnp.logical_not(owner))
        def _():
            arrivals(seen, tiles, reduce_send.at[2 * phase]).wait()

    @pl.when(section > 0)
    def _():
        add_block(slice(None))

    for j in range(tiles):
        p_packed[j] = packed(p_part[:, 2 * LANES * j : 2 * LANES * (j + 1)])
    exchange(p_packed, p_seen, p_total, 0, lambda: None, lambda tile, extra: tile)

    def unpacked(first, count):
        halves = [p_total[j] for j in range(first, first + count)]
        return jnp.concatenate([half for tile in halves for half in (tile[:8].astype(F32), tile[8:].astype(F32))], axis=1)

    p_value = unpacked(0, value_tiles)
    p_out = unpacked(value_tiles, out_tiles)
    p_all[:, :dw] = p_value
    p_all[:, dw:] = p_out
    p_value, p_out = p_value.astype(BF16), p_out.astype(BF16)
    q_value = small_mm(mm_nt(p_value, normed[...]) * scale, value_grad[...]) + mm(p_value, err_value[...])
    for j in range(out_tiles):
        q_packed[j] = packed(q_value[:, 2 * LANES * j : 2 * LANES * (j + 1)])
    q_out = small_mm(mm_nt(p_out, values[...]) * scale, grads[...]) + mm(p_out, err_out[...])
    for j in range(value_tiles):
        q_packed[out_tiles + j] = packed(q_out[:, 2 * LANES * j : 2 * LANES * (j + 1)])

    def factors():
        grams = [
            lax.dot_general(
                x, x, (((1,), (1,)), ((), ())), precision=lax.Precision.HIGHEST, preferred_element_type=F32
            )
            for x in (p_all[:, :dw], p_all[:, dw:])
        ]
        return [inverse_factor(gram) for gram in grams]

    def solved(pair, extra):
        for_value, for_out = extra
        lower = jnp.where(chip < out_tiles, for_value, for_out)
        return jnp.concatenate([apply_small(lower, pair[:8]), apply_small(lower, pair[8:])], axis=0)

    exchange(q_packed, q_seen, q_total, 1, factors, solved)
    out_ref[...] = q_total[...]
    finish_sends(p_seen, 0)
    finish_sends(q_seen, 1)

    @pl.when(section > 0)
    def _():
        def sent(b):
            for c in range(pieces):
                hop(b, c).wait_send()

        each_block(sent)


def part_kernel(both, out_value, out_out):
    out_tiles = out_value.shape[1] // (2 * LANES)
    for j in range(both.shape[0]):
        ref, place = (out_value, j) if j < out_tiles else (out_out, j - out_tiles)
        tile = both[j].astype(F32)
        half = tile.shape[0] // 2
        ref[:, 2 * LANES * place : 2 * LANES * place + LANES] = tile[:half]
        ref[:, 2 * LANES * place + LANES : 2 * LANES * (place + 1)] = tile[half:]


def solution(mesh):
    sections, replicas = mesh.shape["section"], mesh.shape["dp"]

    def shards(
        acts, out_grad, tok_count, norm_gain, w_value, w_out, err_value, err_out, start_q_value, start_q_out
    ):
        rows, dw = out_grad.shape
        hv, rank = start_q_value.shape[1:]
        tiles = (dw + hv) // (2 * LANES)
        blocks = rows // 16
        cuts = tuple(cut * dw // CUTS[-1] for cut in CUTS)
        any_space = pl.BlockSpec(memory_space=pl.ANY)
        vmem = pl.BlockSpec(memory_space=pltpu.VMEM)
        both = pl.pallas_call(
            functools.partial(kernel, sections, replicas, blocks, cuts, GROUPS),
            out_shape=pltpu.VMEM((tiles, 2 * rank, LANES), BF16),
            in_specs=[any_space] * 2 + [pl.BlockSpec(memory_space=pltpu.SMEM)] + [any_space] * 7,
            out_specs=vmem,
            scratch_shapes=[
                pltpu.VMEM((rows, dw), BF16),
                pltpu.VMEM((rows, dw), BF16),
                pltpu.VMEM((1, dw), F32),
                pltpu.VMEM((dw, hv), BF16),
                pltpu.VMEM((hv, dw), BF16),
                pltpu.VMEM((dw, hv), BF16),
                pltpu.VMEM((hv, dw), BF16),
                pltpu.VMEM((rank, hv), F32),
                pltpu.VMEM((rank, dw), F32),
                pltpu.VMEM((hv, dw), BF16),
                pltpu.VMEM((dw, hv), BF16),
                pltpu.VMEM((rows, dw), F32),
                pltpu.VMEM((rows, LANES), F32),
                pltpu.VMEM((rows, dw), BF16),
                pltpu.VMEM((rows, hv), BF16),
                pltpu.VMEM((rows, hv), F32),
                pltpu.VMEM((rows, dw), BF16),
                pltpu.VMEM((rows, dw), BF16),
                pltpu.VMEM((rows, hv), BF16),
                pltpu.VMEM((rows, dw), F32),
                pltpu.VMEM((rank, dw + hv), F32),
                pltpu.VMEM((rank, dw + hv), F32),
                pltpu.VMEM((tiles, 2 * rank, LANES), BF16),
                pltpu.VMEM((tiles, 2 * rank, LANES), BF16),
                pltpu.VMEM((tiles, 2 * rank, LANES), BF16),
                pltpu.VMEM((tiles, 2 * rank, LANES), BF16),
                pltpu.VMEM((replicas, 2 * rank, LANES), BF16),
                pltpu.VMEM((replicas, 2 * rank, LANES), BF16),
                pltpu.SemaphoreType.DMA((9,)),
                pltpu.SemaphoreType.DMA((blocks * (len(cuts) - 1),)),
                pltpu.SemaphoreType.DMA((blocks * (len(cuts) - 1),)),
                pltpu.SemaphoreType.DMA((4,)),
                pltpu.SemaphoreType.DMA((4,)),
            ],
            compiler_params=pltpu.CompilerParams(
                collective_id=0, has_side_effects=True, vmem_limit_bytes=60 * 2**20
            ),
            cost_estimate=pl.CostEstimate(flops=1_700_000_000, bytes_accessed=12_000_000, transcendentals=0),
        )(
            acts[0],
            out_grad,
            tok_count,
            norm_gain,
            w_value[0],
            w_out[0],
            err_value[0],
            err_out[0],
            start_q_value[0].T,
            start_q_out[0].T,
        )
        q_value, q_out = pl.pallas_call(
            part_kernel,
            out_shape=(
                jax.ShapeDtypeStruct((rank, hv), F32),
                jax.ShapeDtypeStruct((rank, dw), F32),
            ),
            in_specs=[vmem],
            out_specs=(vmem, vmem),
        )(both)
        return q_value.T[None], q_out.T[None]

    placed = (
        P("section", "dp", None),
        P("dp", None),
        P("dp"),
        P("section", None),
        P("section", None, None),
        P("section", None, None),
        P("section", "dp", None),
        P("section", "dp", None),
        P("section", None, None),
        P("section", None, None),
    )
    return jax.shard_map(
        shards,
        mesh=mesh,
        in_specs=placed,
        out_specs=(P("section", None, None), P("section", None, None)),
        check_vma=False,
    )
```

```python
import functools

import jax
import jax.numpy as jnp
from jax import lax
from jax.experimental import pallas as pl
from jax.experimental.pallas import tpu as pltpu
from jax.sharding import PartitionSpec as P

EPSILON = 1e-06
LANES = 128
CUTS = (0, 5, 10, 15, 20)
GROUPS = ((0,), (1,), (2,), (3,))
LIFTED = 2
BF16 = jnp.bfloat16
F32 = jnp.float32


def mm(a, b):
    return lax.dot_general(a, b, (((1,), (0,)), ((), ())), preferred_element_type=F32)


def mm_nt(a, b):
    return lax.dot_general(a, b, (((1,), (1,)), ((), ())), preferred_element_type=F32)


def split(x):
    high = x.astype(BF16).astype(F32)
    return jnp.concatenate([high, x - high], axis=0).astype(BF16)


def joined(product):
    half = product.shape[0] // 2
    return product[:half] + product[half:]


def small_mm(x, big):
    return joined(mm(split(x), big))


def small_mm_nt(x, big):
    return joined(mm_nt(split(x), big))


def inverse_factor(gram):
    n = gram.shape[0]
    row = lax.broadcasted_iota(jnp.int32, (n, n), 0)
    col = lax.broadcasted_iota(jnp.int32, (n, n), 1)
    work = jnp.concatenate([gram, jnp.where(row == col, 1.0, 0.0)], axis=1)
    line = lax.broadcasted_iota(jnp.int32, (n, 2 * n), 0)
    for k in range(n):
        root = lax.rsqrt(work[k : k + 1, k : k + 1])
        pivot = work[k : k + 1, :] * root
        factor = work[:, k : k + 1] * root
        work = jnp.where(line == k, pivot, jnp.where(line > k, work - factor * pivot, work))
    return work[:, n:]


def apply_small(lower, tile):
    total = lower[:, 0:1] * tile[0:1, :]
    for k in range(1, lower.shape[1]):
        total = total + lower[:, k : k + 1] * tile[k : k + 1, :]
    return total


def kernel(
    sections,
    replicas,
    blocks,
    cuts,
    groups,
    acts_hbm,
    top_hbm,
    count_ref,
    gain_hbm,
    w_value_hbm,
    w_out_hbm,
    err_value_hbm,
    err_out_hbm,
    q_value_hbm,
    q_out_hbm,
    out_ref,
    acts,
    top,
    gain,
    w_value,
    w_out,
    err_value,
    err_out,
    start_value,
    start_out,
    w_value_t,
    w_out_t,
    unit,
    inv_rms,
    normed,
    values,
    values_wide,
    grads,
    passed,
    value_grad,
    norm_grad,
    p_part,
    p_all,
    p_packed,
    q_packed,
    p_total,
    q_total,
    p_seen,
    q_seen,
    load_sem,
    relay_send,
    relay_recv,
    reduce_send,
    reduce_recv,
    lower_normed,
    lower_values,
    lower_value_q,
    lower_out_q,
    lower_part,
    lower_packed,
    lower_seen,
    lower_total,
    value_q,
    lift_send,
    lift_recv,
):
    section = lax.axis_index("section")
    me = lax.axis_index("dp")
    rows, dw = acts.shape
    hv = w_out.shape[0]
    size = rows // blocks
    value_tiles, out_tiles = dw // (2 * LANES), hv // (2 * LANES)
    tiles = value_tiles + out_tiles
    last = sections - 1
    chips = replicas // 2
    chip, core = me // 2, lax.rem(me, 2)
    owner = (core == 1) & (chip < tiles)
    lifted = section < LIFTED
    lifts = (section > 0) & (section <= LIFTED)
    pieces = len(cuts) - 1

    loads = [
        pltpu.make_async_copy(src, dst, load_sem.at[i])
        for i, (src, dst) in enumerate(
            [
                (top_hbm, top),
                (w_out_hbm, w_out),
                (acts_hbm, acts),
                (gain_hbm, gain),
                (w_value_hbm, w_value),
                (q_value_hbm, start_value),
                (q_out_hbm, start_out),
                (err_value_hbm, err_value),
                (err_out_hbm, err_out),
            ]
        )
    ]
    (l_top, l_w_out, l_acts, l_gain, l_w_value, l_q_value, l_q_out, l_err_value, l_err_out) = loads
    for load in loads[:4]:
        load.start()

    barrier = pltpu.get_barrier_semaphore()

    def greet(k, carry):
        pl.semaphore_signal(
            barrier, inc=1, device_id={"dp": lax.rem(me + k, replicas)}, device_id_type=pl.DeviceIdType.MESH
        )
        return carry

    for step in (1, sections - 1):
        pl.semaphore_signal(
            barrier,
            inc=1,
            device_id={"section": lax.rem(section + step, sections)},
            device_id_type=pl.DeviceIdType.MESH,
        )
    lax.fori_loop(1, replicas, greet, 0)

    @pl.when(lifted)
    def _():
        def greet_owner(k, carry):
            pl.semaphore_signal(
                barrier,
                inc=1,
                device_id={"section": section + 1, "dp": 2 * k + 1},
                device_id_type=pl.DeviceIdType.MESH,
            )
            return carry

        lax.fori_loop(0, tiles, greet_owner, 0)

    def all_here():
        @pl.when(owner & lifts)
        def _():
            pl.semaphore_wait(barrier, 2 * replicas + 1)

        @pl.when(jnp.logical_not(owner & lifts))
        def _():
            pl.semaphore_wait(barrier, replicas + 1)

    count = count_ref[0]
    scale = 1.0 / jnp.full((1, 1), count, jnp.int32).astype(F32)

    def block_rows(b):
        return pl.ds(pl.multiple_of(b * size, size), size)

    def normalise(b):
        here = block_rows(b)
        wide = acts[here, :].astype(F32)
        inv = lax.rsqrt(jnp.mean(wide * wide, axis=-1, keepdims=True) + EPSILON)
        unit_rows = wide * inv
        inv_rms[here, :] = jnp.broadcast_to(inv, (size, LANES))
        unit[here, :] = unit_rows
        normed[here, :] = (unit_rows * gain[...]).astype(BF16)

    def each_block(work):
        def body(b, carry):
            work(b)
            return carry

        lax.fori_loop(0, blocks, body, 0)

    def error_parts():
        p_part[:, :dw] = small_mm_nt(start_value[...], err_value[...])
        p_part[:, dw:] = small_mm_nt(start_out[...], err_out[...])

    def add_block(here):
        p_part[:, :dw] += small_mm(small_mm_nt(start_value[...], value_grad[here, :]) * scale, normed[here, :])
        p_part[:, dw:] += small_mm(small_mm_nt(start_out[...], grads[here, :]) * scale, values[here, :])

    def add_lower(here):
        along = small_mm_nt(lower_value_q[...], passed[here, :]) * scale
        lower_part[:, :dw] += small_mm(along, lower_normed[here, :])
        along = small_mm_nt(lower_out_q[...], passed[here, :]) * scale
        lower_part[:, dw:] += small_mm(along, lower_values[here, :])

    def lift(i):
        src, dst = [
            (normed, lower_normed),
            (values, lower_values),
            (value_q, lower_value_q),
            (start_out, lower_out_q),
            (p_part, lower_part),
        ][i]
        return pltpu.make_async_remote_copy(
            src_ref=src,
            dst_ref=dst,
            send_sem=lift_send.at[i],
            recv_sem=lift_recv.at[i],
            device_id={"section": lax.rem(section + 1, sections)},
            device_id_type=pl.DeviceIdType.MESH,
        )

    def piece(c):
        return slice(cuts[c], cuts[c + 1])

    def hop(b, c):
        return pltpu.make_async_remote_copy(
            src_ref=passed.at[block_rows(b), piece(c)],
            dst_ref=grads.at[block_rows(b), piece(c)],
            send_sem=relay_send.at[b * pieces + c],
            recv_sem=relay_recv.at[b * pieces + c],
            device_id={"section": lax.rem(section + last, sections)},
            device_id_type=pl.DeviceIdType.MESH,
        )

    def pass_on(b, mean, product):
        here = block_rows(b)
        inv = inv_rms[here, 0:1]
        for c in range(pieces):
            cols = piece(c)
            centred = product(cols) * gain[:, cols] - unit[here, cols] * mean
            passed[here, cols] = (grads[here, cols].astype(F32) + inv * centred).astype(BF16)
            if c + 1 == 2:
                for early in range(2):
                    hop(b, early).start()
        for c in range(2, pieces):
            hop(b, c).start()

    def project():
        wide = mm(normed[...], w_value[...])
        values_wide[...] = wide
        values[...] = wide.astype(BF16)

    @pl.when(section == last)
    def _():
        l_top.wait()
        l_w_value.start()
        live = lax.broadcasted_iota(jnp.int32, (rows, 1), 0) < count
        grads[...] = jnp.where(live, top[...].astype(F32), 0.0).astype(BF16)
        l_w_out.wait()
        value_grad[...] = mm_nt(grads[...], w_out[...]).astype(BF16)
        l_acts.wait()
        l_gain.wait()
        l_w_value.wait()
        for load in loads[5:]:
            load.start()
        norm_grad[...] = mm_nt(value_grad[...], w_value[...])
        all_here()

        def send(b):
            here = block_rows(b)
            normalise(b)
            mean = jnp.mean(norm_grad[here, :] * gain[...] * unit[here, :], axis=-1, keepdims=True)
            pass_on(b, mean, lambda cols: norm_grad[here, cols])

        each_block(send)
        project()
        for load in loads[5:]:
            load.wait()
        error_parts()

    @pl.when(section < last)
    def _():
        l_acts.wait()
        l_w_value.start()
        l_gain.wait()
        for load in loads[5:]:
            load.start()
        each_block(normalise)
        l_w_out.wait()
        w_out_t[...] = w_out[...].T
        l_w_value.wait()
        w_value_t[...] = w_value[...].T
        project()
        all_here()


        @pl.when(lifted)
        def _():
            lift(0).start()
            lift(1).start()

        for load in (l_top, *loads[5:]):
            load.wait()

        @pl.when(section < last - 1)
        def _():
            error_parts()

        @pl.when(lifted)
        def _():
            value_q[...] = small_mm(start_value[...], w_out[...])
            for i in range(2, 5):
                lift(i).start()

        def relay(b):
            here = block_rows(b)

            total = None
            for group in groups:
                for c in group:
                    hop(b, c).wait_recv()
                cols = slice(cuts[group[0]], cuts[group[-1] + 1])
                term = mm(grads[here, cols], w_out_t[cols, :])
                total = term if total is None else total + term
            v_rows = total.astype(BF16)
            value_grad[here, :] = v_rows

            @pl.when(section > 0)
            def _():
                mean = jnp.sum(v_rows.astype(F32) * values_wide[here, :], axis=-1, keepdims=True) * (1.0 / dw)
                pass_on(b, mean, lambda cols: mm(v_rows, w_value_t[:, cols]))

        each_block(relay)

        @pl.when(section == last - 1)
        def _():
            error_parts()

    def packed(x):
        return jnp.concatenate([x[:, :LANES], x[:, LANES:]], axis=0).astype(BF16)

    def arrivals(ref, amount, sem):
        return pltpu.make_async_copy(ref.at[pl.ds(0, amount)], ref.at[pl.ds(0, amount)], sem)

    def far_first(k):
        return lax.rem(chip + chips // 2 + 2 + k, chips)

    def scatter(part, seen, phase):
        def body(k, carry):
            to = far_first(k)

            @pl.when((to < tiles) & ((to != chip) | (core == 0)))
            def _():
                pltpu.make_async_remote_copy(
                    src_ref=part.at[to],
                    dst_ref=seen.at[me],
                    send_sem=reduce_send.at[2 * phase],
                    recv_sem=reduce_recv.at[2 * phase],
                    device_id={"dp": 2 * to + 1},
                    device_id_type=pl.DeviceIdType.MESH,
                ).start()

            return carry

        lax.fori_loop(0, chips, body, 0)

    def summed(part, seen, phase):
        seen[me] = part[chip]
        arrivals(seen, replicas - 1, reduce_recv.at[2 * phase]).wait()
        return jnp.sum(seen[...].astype(F32), axis=0)

    def spread(source, total, phase, arrival, to_section, to_self):
        def body(k, carry):
            to = far_first(k)
            for end in range(2):

                @pl.when((to != chip) | (end == 0) | to_self)
                def _():
                    pltpu.make_async_remote_copy(
                        src_ref=source.at[chip],
                        dst_ref=total.at[chip],
                        send_sem=reduce_send.at[2 * phase + 1],
                        recv_sem=reduce_recv.at[arrival],
                        device_id={"section": to_section, "dp": 2 * to + end},
                        device_id_type=pl.DeviceIdType.MESH,
                    ).start()

            return carry

        lax.fori_loop(0, chips, body, 0)

    def gathered(total, phase):
        @pl.when(owner)
        def _():
            arrivals(total, tiles - 1, reduce_recv.at[2 * phase + 1]).wait()

        @pl.when(jnp.logical_not(owner))
        def _():
            arrivals(total, tiles, reduce_recv.at[2 * phase + 1]).wait()

    def pack_all(part, ref):
        for j in range(tiles):
            ref[j] = packed(part[:, 2 * LANES * j : 2 * LANES * (j + 1)])

    def finish_sends(seen, phase):
        @pl.when(owner)
        def _():
            arrivals(seen, tiles - 1, reduce_send.at[2 * phase]).wait()
            arrivals(seen, replicas - 1, reduce_send.at[2 * phase + 1]).wait()

        @pl.when(jnp.logical_not(owner))
        def _():
            arrivals(seen, tiles, reduce_send.at[2 * phase]).wait()

    @pl.when(lifts)
    def _():
        for i in range(5):
            lift(i).wait_recv()
        add_lower(slice(None))

        pack_all(lower_part, lower_packed)
        scatter(lower_packed, lower_seen, 2)

    @pl.when(jnp.logical_not(lifted))
    def _():
        add_block(slice(None))
        pack_all(p_part, p_packed)
        scatter(p_packed, p_seen, 0)

    @pl.when(lifts & owner)
    def _():
        lower_total[chip] = summed(lower_packed, lower_seen, 2).astype(BF16)
        spread(lower_total, p_total, 2, 1, section - 1, True)

    @pl.when(jnp.logical_not(lifted) & owner)
    def _():
        p_total[chip] = summed(p_packed, p_seen, 0).astype(BF16)
        spread(p_total, p_total, 0, 1, section, False)

    @pl.when(jnp.logical_not(lifted))
    def _():
        gathered(p_total, 0)

    @pl.when(lifted)
    def _():
        arrivals(p_total, tiles, reduce_recv.at[1]).wait()

    def unpacked(first, count):
        halves = [p_total[j] for j in range(first, first + count)]
        return jnp.concatenate([half for tile in halves for half in (tile[:8].astype(F32), tile[8:].astype(F32))], axis=1)

    p_value = unpacked(0, value_tiles)
    p_out = unpacked(value_tiles, out_tiles)
    p_all[:, :dw] = p_value
    p_all[:, dw:] = p_out
    p_value, p_out = p_value.astype(BF16), p_out.astype(BF16)
    q_value = small_mm(mm_nt(p_value, normed[...]) * scale, value_grad[...]) + mm(p_value, err_value[...])
    for j in range(out_tiles):
        q_packed[j] = packed(q_value[:, 2 * LANES * j : 2 * LANES * (j + 1)])
    q_out = small_mm(mm_nt(p_out, values[...]) * scale, grads[...]) + mm(p_out, err_out[...])
    for j in range(value_tiles):
        q_packed[out_tiles + j] = packed(q_out[:, 2 * LANES * j : 2 * LANES * (j + 1)])

    def factors():
        grams = [
            lax.dot_general(
                x, x, (((1,), (1,)), ((), ())), precision=lax.Precision.HIGHEST, preferred_element_type=F32
            )
            for x in (p_all[:, :dw], p_all[:, dw:])
        ]
        return [inverse_factor(gram) for gram in grams]

    def solved(pair, extra):
        for_value, for_out = extra
        lower = jnp.where(chip < out_tiles, for_value, for_out)
        return jnp.concatenate([apply_small(lower, pair[:8]), apply_small(lower, pair[8:])], axis=0)

    scatter(q_packed, q_seen, 1)
    extra = factors()

    @pl.when(owner)
    def _():
        q_total[chip] = solved(summed(q_packed, q_seen, 1), extra).astype(BF16)
        spread(q_total, q_total, 1, 3, section, False)

    gathered(q_total, 1)
    out_ref[...] = q_total[...]
    finish_sends(q_seen, 1)

    @pl.when(jnp.logical_not(lifted))
    def _():
        finish_sends(p_seen, 0)

    @pl.when(lifts)
    def _():
        @pl.when(owner)
        def _():
            arrivals(lower_seen, tiles - 1, reduce_send.at[4]).wait()
            arrivals(lower_seen, replicas, reduce_send.at[5]).wait()

        @pl.when(jnp.logical_not(owner))
        def _():
            arrivals(lower_seen, tiles, reduce_send.at[4]).wait()

    @pl.when(section > 0)
    def _():
        def sent(b):
            for c in range(pieces):
                hop(b, c).wait_send()

        each_block(sent)

    @pl.when(lifted)
    def _():
        for i in range(5):
            lift(i).wait_send()


def part_kernel(both, out_value, out_out):
    out_tiles = out_value.shape[1] // (2 * LANES)
    for j in range(both.shape[0]):
        ref, place = (out_value, j) if j < out_tiles else (out_out, j - out_tiles)
        tile = both[j].astype(F32)
        half = tile.shape[0] // 2
        ref[:, 2 * LANES * place : 2 * LANES * place + LANES] = tile[:half]
        ref[:, 2 * LANES * place + LANES : 2 * LANES * (place + 1)] = tile[half:]


def solution(mesh):
    sections, replicas = mesh.shape["section"], mesh.shape["dp"]

    def shards(
        acts, out_grad, tok_count, norm_gain, w_value, w_out, err_value, err_out, start_q_value, start_q_out
    ):
        rows, dw = out_grad.shape
        hv, rank = start_q_value.shape[1:]
        tiles = (dw + hv) // (2 * LANES)
        blocks = rows // 16
        cuts = tuple(cut * dw // CUTS[-1] for cut in CUTS)
        any_space = pl.BlockSpec(memory_space=pl.ANY)
        vmem = pl.BlockSpec(memory_space=pltpu.VMEM)
        both = pl.pallas_call(
            functools.partial(kernel, sections, replicas, blocks, cuts, GROUPS),
            out_shape=pltpu.VMEM((tiles, 2 * rank, LANES), BF16),
            in_specs=[any_space] * 2 + [pl.BlockSpec(memory_space=pltpu.SMEM)] + [any_space] * 7,
            out_specs=vmem,
            scratch_shapes=[
                pltpu.VMEM((rows, dw), BF16),
                pltpu.VMEM((rows, dw), BF16),
                pltpu.VMEM((1, dw), F32),
                pltpu.VMEM((dw, hv), BF16),
                pltpu.VMEM((hv, dw), BF16),
                pltpu.VMEM((dw, hv), BF16),
                pltpu.VMEM((hv, dw), BF16),
                pltpu.VMEM((rank, hv), F32),
                pltpu.VMEM((rank, dw), F32),
                pltpu.VMEM((hv, dw), BF16),
                pltpu.VMEM((dw, hv), BF16),
                pltpu.VMEM((rows, dw), F32),
                pltpu.VMEM((rows, LANES), F32),
                pltpu.VMEM((rows, dw), BF16),
                pltpu.VMEM((rows, hv), BF16),
                pltpu.VMEM((rows, hv), F32),
                pltpu.VMEM((rows, dw), BF16),
                pltpu.VMEM((rows, dw), BF16),
                pltpu.VMEM((rows, hv), BF16),
                pltpu.VMEM((rows, dw), F32),
                pltpu.VMEM((rank, dw + hv), F32),
                pltpu.VMEM((rank, dw + hv), F32),
                pltpu.VMEM((tiles, 2 * rank, LANES), BF16),
                pltpu.VMEM((tiles, 2 * rank, LANES), BF16),
                pltpu.VMEM((tiles, 2 * rank, LANES), BF16),
                pltpu.VMEM((tiles, 2 * rank, LANES), BF16),
                pltpu.VMEM((replicas, 2 * rank, LANES), BF16),
                pltpu.VMEM((replicas, 2 * rank, LANES), BF16),
                pltpu.SemaphoreType.DMA((9,)),
                pltpu.SemaphoreType.DMA((blocks * (len(cuts) - 1),)),
                pltpu.SemaphoreType.DMA((blocks * (len(cuts) - 1),)),
                pltpu.SemaphoreType.DMA((6,)),
                pltpu.SemaphoreType.DMA((6,)),
                pltpu.VMEM((rows, dw), BF16),
                pltpu.VMEM((rows, hv), BF16),
                pltpu.VMEM((rank, dw), F32),
                pltpu.VMEM((rank, dw), F32),
                pltpu.VMEM((rank, dw + hv), F32),
                pltpu.VMEM((tiles, 2 * rank, LANES), BF16),
                pltpu.VMEM((replicas, 2 * rank, LANES), BF16),
                pltpu.VMEM((tiles, 2 * rank, LANES), BF16),
                pltpu.VMEM((rank, dw), F32),
                pltpu.SemaphoreType.DMA((5,)),
                pltpu.SemaphoreType.DMA((5,)),
            ],
            compiler_params=pltpu.CompilerParams(
                collective_id=0, has_side_effects=True, vmem_limit_bytes=60 * 2**20
            ),
            cost_estimate=pl.CostEstimate(flops=1_700_000_000, bytes_accessed=12_000_000, transcendentals=0),
        )(
            acts[0],
            out_grad,
            tok_count,
            norm_gain,
            w_value[0],
            w_out[0],
            err_value[0],
            err_out[0],
            start_q_value[0].T,
            start_q_out[0].T,
        )
        q_value, q_out = pl.pallas_call(
            part_kernel,
            out_shape=(
                jax.ShapeDtypeStruct((rank, hv), F32),
                jax.ShapeDtypeStruct((rank, dw), F32),
            ),
            in_specs=[vmem],
            out_specs=(vmem, vmem),
        )(both)
        return q_value.T[None], q_out.T[None]

    placed = (
        P("section", "dp", None),
        P("dp", None),
        P("dp"),
        P("section", None),
        P("section", None, None),
        P("section", None, None),
        P("section", "dp", None),
        P("section", "dp", None),
        P("section", None, None),
        P("section", None, None),
    )
    return jax.shard_map(
        shards,
        mesh=mesh,
        in_specs=placed,
        out_specs=(P("section", None, None), P("section", None, None)),
        check_vma=False,
    )
```

```python
import functools
import math

import jax
import jax.numpy as jnp
from jax import lax
from jax.experimental import pallas as pl
from jax.experimental.pallas import tpu as pltpu
from jax.sharding import PartitionSpec as P

EPSILON = 1e-06
LANES = 128
CUTS = (0, 5, 10, 15, 20)
GROUPS = ((0,), (1,), (2,), (3,))
LIFTED = 2
BF16 = jnp.bfloat16
F32 = jnp.float32


def mm(a, b):
    return lax.dot_general(a, b, (((1,), (0,)), ((), ())), preferred_element_type=F32)


def mm_nt(a, b):
    return lax.dot_general(a, b, (((1,), (1,)), ((), ())), preferred_element_type=F32)


def split(x):
    high = x.astype(BF16).astype(F32)
    return jnp.concatenate([high, x - high], axis=0).astype(BF16)


def joined(product):
    half = product.shape[0] // 2
    return product[:half] + product[half:]


def small_mm(x, big):
    return joined(mm(split(x), big))


def small_mm_nt(x, big):
    return joined(mm_nt(split(x), big))


def inverse_factor(gram):
    n = gram.shape[0]
    row = lax.broadcasted_iota(jnp.int32, (n, n), 0)
    col = lax.broadcasted_iota(jnp.int32, (n, n), 1)
    work = jnp.concatenate([gram, jnp.where(row == col, 1.0, 0.0)], axis=1)
    line = lax.broadcasted_iota(jnp.int32, (n, 2 * n), 0)
    for k in range(n):
        root = lax.rsqrt(work[k : k + 1, k : k + 1])
        pivot = work[k : k + 1, :] * root
        factor = work[:, k : k + 1] * root
        work = jnp.where(line == k, pivot, jnp.where(line > k, work - factor * pivot, work))
    return work[:, n:]


def apply_small(lower, tile):
    total = lower[:, 0:1] * tile[0:1, :]
    for k in range(1, lower.shape[1]):
        total = total + lower[:, k : k + 1] * tile[k : k + 1, :]
    return total


def kernel(
    sections,
    replicas,
    blocks,
    cuts,
    groups,
    acts_hbm,
    top_hbm,
    count_ref,
    gain_hbm,
    w_value_hbm,
    w_out_hbm,
    err_value_hbm,
    err_out_hbm,
    q_value_hbm,
    q_out_hbm,
    out_value,
    out_out,
    acts,
    top,
    gain,
    w_value,
    w_out,
    err_value,
    err_out,
    start_value,
    start_out,
    w_value_t,
    w_out_t,
    unit,
    inv_rms,
    normed,
    values,
    values_wide,
    grads,
    passed,
    value_grad,
    norm_grad,
    p_part,
    p_all,
    p_packed,
    q_packed,
    p_total,
    q_total,
    p_seen,
    q_seen,
    load_sem,
    relay_send,
    relay_recv,
    reduce_send,
    reduce_recv,
    lower_normed,
    lower_values,
    lower_value_q,
    lower_out_q,
    lower_part,
    lower_packed,
    lower_seen,
    lower_total,
    value_q,
    normed_t,
    lift_send,
    lift_recv,
):
    section = lax.axis_index("section")
    me = lax.axis_index("dp")
    rows, dw = acts.shape
    hv = w_out.shape[0]
    size = rows // blocks
    value_tiles, out_tiles = dw // (2 * LANES), hv // (2 * LANES)
    tiles = value_tiles + out_tiles
    last = sections - 1
    chips = replicas // 2
    chip, core = me // 2, lax.rem(me, 2)
    owner = (core == 1) & (chip < tiles)
    lifted = section < LIFTED
    lifts = (section > 0) & (section <= LIFTED)
    pieces = len(cuts) - 1

    loads = [
        pltpu.make_async_copy(src, dst, load_sem.at[i])
        for i, (src, dst) in enumerate(
            [
                (top_hbm, top),
                (w_out_hbm, w_out),
                (acts_hbm, acts),
                (gain_hbm, gain),
                (w_value_hbm, w_value),
                (q_value_hbm, start_value),
                (q_out_hbm, start_out),
                (err_value_hbm, err_value),
                (err_out_hbm, err_out),
            ]
        )
    ]
    (l_top, l_w_out, l_acts, l_gain, l_w_value, l_q_value, l_q_out, l_err_value, l_err_out) = loads
    for load in loads[:4]:
        load.start()

    barrier = pltpu.get_barrier_semaphore()

    def greet(k, carry):
        pl.semaphore_signal(
            barrier, inc=1, device_id={"dp": lax.rem(me + k, replicas)}, device_id_type=pl.DeviceIdType.MESH
        )
        return carry

    for step in (1, sections - 1):
        pl.semaphore_signal(
            barrier,
            inc=1,
            device_id={"section": lax.rem(section + step, sections)},
            device_id_type=pl.DeviceIdType.MESH,
        )
    lax.fori_loop(1, replicas, greet, 0)

    @pl.when(lifted)
    def _():
        def greet_owner(k, carry):
            pl.semaphore_signal(
                barrier,
                inc=1,
                device_id={"section": section + 1, "dp": 2 * k + 1},
                device_id_type=pl.DeviceIdType.MESH,
            )
            return carry

        lax.fori_loop(0, tiles, greet_owner, 0)

    def all_here():
        @pl.when(owner & lifts)
        def _():
            pl.semaphore_wait(barrier, 2 * replicas + 1)

        @pl.when(jnp.logical_not(owner & lifts))
        def _():
            pl.semaphore_wait(barrier, replicas + 1)

    count = count_ref[0]
    scale = 1.0 / jnp.full((1, 1), count, jnp.int32).astype(F32)

    def block_rows(b):
        return pl.ds(pl.multiple_of(b * size, size), size)

    def normalise(b):
        here = block_rows(b)
        wide = acts[here, :].astype(F32)
        inv = lax.rsqrt(jnp.mean(wide * wide, axis=-1, keepdims=True) + EPSILON)
        unit_rows = wide * inv
        inv_rms[here, :] = jnp.broadcast_to(inv, (size, LANES))
        unit[here, :] = unit_rows
        normed[here, :] = (unit_rows * gain[...]).astype(BF16)

    def each_block(work):
        def body(b, carry):
            work(b)
            return carry

        lax.fori_loop(0, blocks, body, 0)

    def error_parts():
        p_part[:, :dw] = small_mm_nt(start_value[...], err_value[...])
        p_part[:, dw:] = small_mm_nt(start_out[...], err_out[...])

    def add_block(here):
        p_part[:, :dw] += small_mm(small_mm_nt(start_value[...], value_grad[here, :]) * scale, normed[here, :])
        p_part[:, dw:] += small_mm(small_mm_nt(start_out[...], grads[here, :]) * scale, values[here, :])

    def add_lower(here):
        along = small_mm_nt(lower_value_q[...], passed[here, :]) * scale
        lower_part[:, :dw] += small_mm(along, lower_normed[here, :])
        along = small_mm_nt(lower_out_q[...], passed[here, :]) * scale
        lower_part[:, dw:] += small_mm(along, lower_values[here, :])

    def lift(i):
        src, dst = [
            (normed, lower_normed),
            (values, lower_values),
            (value_q, lower_value_q),
            (start_out, lower_out_q),
            (p_part, lower_part),
        ][i]
        return pltpu.make_async_remote_copy(
            src_ref=src,
            dst_ref=dst,
            send_sem=lift_send.at[i],
            recv_sem=lift_recv.at[i],
            device_id={"section": lax.rem(section + 1, sections)},
            device_id_type=pl.DeviceIdType.MESH,
        )

    def piece(c):
        return slice(cuts[c], cuts[c + 1])

    def hop(b, c):
        return pltpu.make_async_remote_copy(
            src_ref=passed.at[block_rows(b), piece(c)],
            dst_ref=grads.at[block_rows(b), piece(c)],
            send_sem=relay_send.at[b * pieces + c],
            recv_sem=relay_recv.at[b * pieces + c],
            device_id={"section": lax.rem(section + last, sections)},
            device_id_type=pl.DeviceIdType.MESH,
        )

    def pass_on(b, mean, product):
        here = block_rows(b)
        inv = inv_rms[here, 0:1]
        for c in range(pieces):
            cols = piece(c)
            centred = product(cols) * gain[:, cols] - unit[here, cols] * mean
            passed[here, cols] = (grads[here, cols].astype(F32) + inv * centred).astype(BF16)
            if c + 1 == 2:
                for early in range(2):
                    hop(b, early).start()
        for c in range(2, pieces):
            hop(b, c).start()

    def project():
        wide = mm(normed[...], w_value[...])
        values_wide[...] = wide
        values[...] = wide.astype(BF16)
        normed_t[...] = normed[...].T

    @pl.when(section == last)
    def _():
        l_top.wait()
        l_w_value.start()
        live = lax.broadcasted_iota(jnp.int32, (rows, 1), 0) < count
        grads[...] = jnp.where(live, top[...].astype(F32), 0.0).astype(BF16)
        l_w_out.wait()
        value_grad[...] = mm_nt(grads[...], w_out[...]).astype(BF16)
        l_acts.wait()
        l_gain.wait()
        l_w_value.wait()
        for load in loads[5:]:
            load.start()
        norm_grad[...] = mm_nt(value_grad[...], w_value[...])
        all_here()

        def send(b):
            here = block_rows(b)
            normalise(b)
            mean = jnp.mean(norm_grad[here, :] * gain[...] * unit[here, :], axis=-1, keepdims=True)
            pass_on(b, mean, lambda cols: norm_grad[here, cols])

        each_block(send)
        project()
        for load in loads[5:]:
            load.wait()
        error_parts()

    @pl.when(section < last)
    def _():
        l_acts.wait()
        l_w_value.start()
        l_gain.wait()
        for load in loads[5:]:
            load.start()
        each_block(normalise)
        l_w_out.wait()
        w_out_t[...] = w_out[...].T
        l_w_value.wait()
        w_value_t[...] = w_value[...].T
        project()
        all_here()


        @pl.when(lifted)
        def _():
            lift(0).start()
            lift(1).start()

        for load in (l_top, *loads[5:]):
            load.wait()

        @pl.when(section < last - 1)
        def _():
            error_parts()

        @pl.when(lifted)
        def _():
            value_q[...] = small_mm(start_value[...], w_out[...])
            for i in range(2, 5):
                lift(i).start()

        def relay(b):
            here = block_rows(b)

            total = None
            for group in groups:
                for c in group:
                    hop(b, c).wait_recv()
                cols = slice(cuts[group[0]], cuts[group[-1] + 1])
                term = mm(grads[here, cols], w_out_t[cols, :])
                total = term if total is None else total + term
            v_rows = total.astype(BF16)
            value_grad[here, :] = v_rows

            @pl.when(section > 0)
            def _():
                mean = jnp.sum(v_rows.astype(F32) * values_wide[here, :], axis=-1, keepdims=True) * (1.0 / dw)
                pass_on(b, mean, lambda cols: mm(v_rows, w_value_t[:, cols]))

        each_block(relay)

        @pl.when(section == last - 1)
        def _():
            error_parts()

    def packed(x):
        return jnp.concatenate([x[:, :LANES], x[:, LANES:]], axis=0).astype(BF16)

    def arrivals(ref, amount, sem):
        return pltpu.make_async_copy(ref.at[pl.ds(0, amount)], ref.at[pl.ds(0, amount)], sem)

    side = math.isqrt(chips) if math.isqrt(chips) ** 2 == chips else 1
    height = chips // side

    def hops(offset):
        return min(offset[0], height - offset[0]) + min(offset[1], side - offset[1])

    offsets = sorted(((dy, dx) for dy in range(height) for dx in range(side)), key=hops, reverse=True)
    farthest_first = [
        (hops(o) == 0, lax.rem(chip // side + o[0], height) * side + lax.rem(lax.rem(chip, side) + o[1], side))
        for o in offsets
    ]

    def scatter(part, seen, phase):
        for here, to in farthest_first:

            @pl.when((to < tiles) & (core == 0) if here else to < tiles)
            def _():
                pltpu.make_async_remote_copy(
                    src_ref=part.at[to],
                    dst_ref=seen.at[me],
                    send_sem=reduce_send.at[2 * phase],
                    recv_sem=reduce_recv.at[2 * phase],
                    device_id={"dp": 2 * to + 1},
                    device_id_type=pl.DeviceIdType.MESH,
                ).start()

    def summed(part, seen, phase):
        seen[me] = part[chip]
        arrivals(seen, replicas - 1, reduce_recv.at[2 * phase]).wait()
        return jnp.sum(seen[...].astype(F32), axis=0)

    def spread(source, total, phase, arrival, to_section, to_self):
        for here, to in farthest_first:
            for end in range(1 if here and not to_self else 2):
                pltpu.make_async_remote_copy(
                    src_ref=source.at[chip],
                    dst_ref=total.at[chip],
                    send_sem=reduce_send.at[2 * phase + 1],
                    recv_sem=reduce_recv.at[arrival],
                    device_id={"section": to_section, "dp": 2 * to + end},
                    device_id_type=pl.DeviceIdType.MESH,
                ).start()

    def gathered(total, phase):
        @pl.when(owner)
        def _():
            arrivals(total, tiles - 1, reduce_recv.at[2 * phase + 1]).wait()

        @pl.when(jnp.logical_not(owner))
        def _():
            arrivals(total, tiles, reduce_recv.at[2 * phase + 1]).wait()

    def pack_all(part, ref):
        for j in range(tiles):
            ref[j] = packed(part[:, 2 * LANES * j : 2 * LANES * (j + 1)])

    def finish_sends(seen, phase):
        @pl.when(owner)
        def _():
            arrivals(seen, tiles - 1, reduce_send.at[2 * phase]).wait()
            arrivals(seen, replicas - 1, reduce_send.at[2 * phase + 1]).wait()

        @pl.when(jnp.logical_not(owner))
        def _():
            arrivals(seen, tiles, reduce_send.at[2 * phase]).wait()

    @pl.when(lifts)
    def _():
        for i in range(5):
            lift(i).wait_recv()
        add_lower(slice(None))

        pack_all(lower_part, lower_packed)
        scatter(lower_packed, lower_seen, 2)

    @pl.when(jnp.logical_not(lifted))
    def _():
        add_block(slice(None))
        pack_all(p_part, p_packed)
        scatter(p_packed, p_seen, 0)

    @pl.when(lifts & owner)
    def _():
        lower_total[chip] = summed(lower_packed, lower_seen, 2).astype(BF16)
        spread(lower_total, p_total, 2, 1, section - 1, True)

    @pl.when(jnp.logical_not(lifted) & owner)
    def _():
        p_total[chip] = summed(p_packed, p_seen, 0).astype(BF16)
        spread(p_total, p_total, 0, 1, section, False)

    @pl.when(jnp.logical_not(lifted))
    def _():
        gathered(p_total, 0)

    @pl.when(lifted)
    def _():
        arrivals(p_total, tiles, reduce_recv.at[1]).wait()

    def unpacked(first, count):
        halves = [p_total[j] for j in range(first, first + count)]
        return jnp.concatenate([half for tile in halves for half in (tile[:8].astype(F32), tile[8:].astype(F32))], axis=1)

    p_value = unpacked(0, value_tiles)
    p_out = unpacked(value_tiles, out_tiles)
    p_all[:, :dw] = p_value
    p_all[:, dw:] = p_out
    p_value, p_out = p_value.astype(BF16), p_out.astype(BF16)
    q_value = small_mm(mm(p_value, normed_t[...]) * scale, value_grad[...]) + mm(p_value, err_value[...])
    for j in range(out_tiles):
        q_packed[j] = packed(q_value[:, 2 * LANES * j : 2 * LANES * (j + 1)])
    q_out = small_mm(mm_nt(p_out, values[...]) * scale, grads[...]) + mm(p_out, err_out[...])
    for j in range(value_tiles):
        q_packed[out_tiles + j] = packed(q_out[:, 2 * LANES * j : 2 * LANES * (j + 1)])

    def factors():
        grams = [
            lax.dot_general(
                x, x, (((1,), (1,)), ((), ())), precision=lax.Precision.HIGHEST, preferred_element_type=F32
            )
            for x in (p_all[:, :dw], p_all[:, dw:])
        ]
        return [inverse_factor(gram) for gram in grams]

    def solved(pair, extra):
        for_value, for_out = extra
        lower = jnp.where(chip < out_tiles, for_value, for_out)
        return jnp.concatenate([apply_small(lower, pair[:8]), apply_small(lower, pair[8:])], axis=0)

    scatter(q_packed, q_seen, 1)
    extra = factors()

    @pl.when(owner)
    def _():
        q_total[chip] = solved(summed(q_packed, q_seen, 1), extra).astype(BF16)
        spread(q_total, q_total, 1, 3, section, False)

    gathered(q_total, 1)
    for j in range(tiles):
        ref, place = (out_value, j) if j < out_tiles else (out_out, j - out_tiles)
        tile = q_total[j].astype(F32)
        ref[:, 2 * LANES * place : 2 * LANES * place + LANES] = tile[:8]
        ref[:, 2 * LANES * place + LANES : 2 * LANES * (place + 1)] = tile[8:]
    finish_sends(q_seen, 1)

    @pl.when(jnp.logical_not(lifted))
    def _():
        finish_sends(p_seen, 0)

    @pl.when(lifts)
    def _():
        @pl.when(owner)
        def _():
            arrivals(lower_seen, tiles - 1, reduce_send.at[4]).wait()
            arrivals(lower_seen, replicas, reduce_send.at[5]).wait()

        @pl.when(jnp.logical_not(owner))
        def _():
            arrivals(lower_seen, tiles, reduce_send.at[4]).wait()

    @pl.when(section > 0)
    def _():
        def sent(b):
            for c in range(pieces):
                hop(b, c).wait_send()

        each_block(sent)

    @pl.when(lifted)
    def _():
        for i in range(5):
            lift(i).wait_send()


def solution(mesh):
    sections, replicas = mesh.shape["section"], mesh.shape["dp"]

    def shards(
        acts, out_grad, tok_count, norm_gain, w_value, w_out, err_value, err_out, start_q_value, start_q_out
    ):
        rows, dw = out_grad.shape
        hv, rank = start_q_value.shape[1:]
        tiles = (dw + hv) // (2 * LANES)
        blocks = rows // 16
        cuts = tuple(cut * dw // CUTS[-1] for cut in CUTS)
        any_space = pl.BlockSpec(memory_space=pl.ANY)
        vmem = pl.BlockSpec(memory_space=pltpu.VMEM)
        q_value, q_out = pl.pallas_call(
            functools.partial(kernel, sections, replicas, blocks, cuts, GROUPS),
            out_shape=(pltpu.VMEM((rank, hv), F32), pltpu.VMEM((rank, dw), F32)),
            in_specs=[any_space] * 2 + [pl.BlockSpec(memory_space=pltpu.SMEM)] + [any_space] * 7,
            out_specs=(vmem, vmem),
            scratch_shapes=[
                pltpu.VMEM((rows, dw), BF16),
                pltpu.VMEM((rows, dw), BF16),
                pltpu.VMEM((1, dw), F32),
                pltpu.VMEM((dw, hv), BF16),
                pltpu.VMEM((hv, dw), BF16),
                pltpu.VMEM((dw, hv), BF16),
                pltpu.VMEM((hv, dw), BF16),
                pltpu.VMEM((rank, hv), F32),
                pltpu.VMEM((rank, dw), F32),
                pltpu.VMEM((hv, dw), BF16),
                pltpu.VMEM((dw, hv), BF16),
                pltpu.VMEM((rows, dw), F32),
                pltpu.VMEM((rows, LANES), F32),
                pltpu.VMEM((rows, dw), BF16),
                pltpu.VMEM((rows, hv), BF16),
                pltpu.VMEM((rows, hv), F32),
                pltpu.VMEM((rows, dw), BF16),
                pltpu.VMEM((rows, dw), BF16),
                pltpu.VMEM((rows, hv), BF16),
                pltpu.VMEM((rows, dw), F32),
                pltpu.VMEM((rank, dw + hv), F32),
                pltpu.VMEM((rank, dw + hv), F32),
                pltpu.VMEM((tiles, 2 * rank, LANES), BF16),
                pltpu.VMEM((tiles, 2 * rank, LANES), BF16),
                pltpu.VMEM((tiles, 2 * rank, LANES), BF16),
                pltpu.VMEM((tiles, 2 * rank, LANES), BF16),
                pltpu.VMEM((replicas, 2 * rank, LANES), BF16),
                pltpu.VMEM((replicas, 2 * rank, LANES), BF16),
                pltpu.SemaphoreType.DMA((9,)),
                pltpu.SemaphoreType.DMA((blocks * (len(cuts) - 1),)),
                pltpu.SemaphoreType.DMA((blocks * (len(cuts) - 1),)),
                pltpu.SemaphoreType.DMA((6,)),
                pltpu.SemaphoreType.DMA((6,)),
                pltpu.VMEM((rows, dw), BF16),
                pltpu.VMEM((rows, hv), BF16),
                pltpu.VMEM((rank, dw), F32),
                pltpu.VMEM((rank, dw), F32),
                pltpu.VMEM((rank, dw + hv), F32),
                pltpu.VMEM((tiles, 2 * rank, LANES), BF16),
                pltpu.VMEM((replicas, 2 * rank, LANES), BF16),
                pltpu.VMEM((tiles, 2 * rank, LANES), BF16),
                pltpu.VMEM((rank, dw), F32),
                pltpu.VMEM((dw, rows), BF16),
                pltpu.SemaphoreType.DMA((5,)),
                pltpu.SemaphoreType.DMA((5,)),
            ],
            compiler_params=pltpu.CompilerParams(
                collective_id=0, has_side_effects=True, vmem_limit_bytes=60 * 2**20
            ),
            cost_estimate=pl.CostEstimate(flops=1_700_000_000, bytes_accessed=12_000_000, transcendentals=0),
        )(
            acts[0],
            out_grad,
            tok_count,
            norm_gain,
            w_value[0],
            w_out[0],
            err_value[0],
            err_out[0],
            start_q_value[0].T,
            start_q_out[0].T,
        )
        return q_value.T[None], q_out.T[None]

    placed = (
        P("section", "dp", None),
        P("dp", None),
        P("dp"),
        P("section", None),
        P("section", None, None),
        P("section", None, None),
        P("section", "dp", None),
        P("section", "dp", None),
        P("section", None, None),
        P("section", None, None),
    )
    return jax.shard_map(
        shards,
        mesh=mesh,
        in_specs=placed,
        out_specs=(P("section", None, None), P("section", None, None)),
        check_vma=False,
    )
```

```python
import functools
import math

import jax
import jax.numpy as jnp
from jax import lax
from jax.experimental import pallas as pl
from jax.experimental.pallas import tpu as pltpu
from jax.sharding import PartitionSpec as P

EPSILON = 1e-06
LANES = 128
CUTS = (0, 5, 10, 15, 20)
GROUPS = ((0,), (1,), (2,), (3,))
LIFTED = 2
BF16 = jnp.bfloat16
F32 = jnp.float32


def mm(a, b):
    return lax.dot_general(a, b, (((1,), (0,)), ((), ())), preferred_element_type=F32)


def mm_nt(a, b):
    return lax.dot_general(a, b, (((1,), (1,)), ((), ())), preferred_element_type=F32)


def split(x):
    high = x.astype(BF16).astype(F32)
    return jnp.concatenate([high, x - high], axis=0).astype(BF16)


def joined(product):
    half = product.shape[0] // 2
    return product[:half] + product[half:]


def small_mm(x, big):
    return joined(mm(split(x), big))


def small_mm_nt(x, big):
    return joined(mm_nt(split(x), big))


def inverse_factor(gram):
    n = gram.shape[0]
    row = lax.broadcasted_iota(jnp.int32, (n, n), 0)
    col = lax.broadcasted_iota(jnp.int32, (n, n), 1)
    work = jnp.concatenate([gram, jnp.where(row == col, 1.0, 0.0)], axis=1)
    line = lax.broadcasted_iota(jnp.int32, (n, 2 * n), 0)
    for k in range(n):
        root = lax.rsqrt(work[k : k + 1, k : k + 1])
        pivot = work[k : k + 1, :] * root
        factor = work[:, k : k + 1] * root
        work = jnp.where(line == k, pivot, jnp.where(line > k, work - factor * pivot, work))
    return work[:, n:]


def apply_small(lower, tile):
    total = lower[:, 0:1] * tile[0:1, :]
    for k in range(1, lower.shape[1]):
        total = total + lower[:, k : k + 1] * tile[k : k + 1, :]
    return total


def kernel(
    sections,
    replicas,
    blocks,
    cuts,
    groups,
    acts_hbm,
    top_hbm,
    count_ref,
    gain_hbm,
    w_value_hbm,
    w_out_hbm,
    err_value_hbm,
    err_out_hbm,
    q_value_hbm,
    q_out_hbm,
    out_value,
    out_out,
    acts,
    top,
    gain,
    w_value,
    w_out,
    err_value,
    err_out,
    start_value,
    start_out,
    w_value_t,
    w_out_t,
    unit,
    inv_rms,
    normed,
    values,
    values_wide,
    grads,
    passed,
    value_grad,
    norm_grad,
    p_part,
    p_all,
    p_packed,
    q_packed,
    p_total,
    q_total,
    p_seen,
    q_seen,
    load_sem,
    relay_send,
    relay_recv,
    reduce_send,
    reduce_recv,
    lower_normed,
    lower_values,
    lower_value_q,
    lower_out_q,
    lower_part,
    lower_packed,
    lower_seen,
    lower_total,
    value_q,
    normed_t,
    lift_send,
    lift_recv,
):
    section = lax.axis_index("section")
    me = lax.axis_index("dp")
    rows, dw = acts.shape
    hv = w_out.shape[0]
    size = rows // blocks
    value_tiles, out_tiles = dw // (2 * LANES), hv // (2 * LANES)
    tiles = value_tiles + out_tiles
    last = sections - 1
    chips = replicas // 2
    chip, core = me // 2, lax.rem(me, 2)
    owner = (core == 1) & (chip < tiles)
    lifted = section < LIFTED
    lifts = (section > 0) & (section <= LIFTED)
    pieces = len(cuts) - 1

    loads = [
        pltpu.make_async_copy(src, dst, load_sem.at[i])
        for i, (src, dst) in enumerate(
            [
                (top_hbm, top),
                (w_out_hbm, w_out),
                (acts_hbm, acts),
                (gain_hbm, gain),
                (w_value_hbm, w_value),
                (q_value_hbm, start_value),
                (q_out_hbm, start_out),
                (err_value_hbm, err_value),
                (err_out_hbm, err_out),
            ]
        )
    ]
    (l_top, l_w_out, l_acts, l_gain, l_w_value, l_q_value, l_q_out, l_err_value, l_err_out) = loads
    for load in loads[:5]:
        load.start()

    barrier = pltpu.get_barrier_semaphore()

    def greet(k, carry):
        pl.semaphore_signal(
            barrier, inc=1, device_id={"dp": lax.rem(me + k, replicas)}, device_id_type=pl.DeviceIdType.MESH
        )
        return carry

    for step in (1, sections - 1):
        pl.semaphore_signal(
            barrier,
            inc=1,
            device_id={"section": lax.rem(section + step, sections)},
            device_id_type=pl.DeviceIdType.MESH,
        )
    lax.fori_loop(1, replicas, greet, 0)

    @pl.when(lifted)
    def _():
        def greet_owner(k, carry):
            pl.semaphore_signal(
                barrier,
                inc=1,
                device_id={"section": section + 1, "dp": 2 * k + 1},
                device_id_type=pl.DeviceIdType.MESH,
            )
            return carry

        lax.fori_loop(0, tiles, greet_owner, 0)

    def all_here():
        @pl.when(owner & lifts)
        def _():
            pl.semaphore_wait(barrier, 2 * replicas + 1)

        @pl.when(jnp.logical_not(owner & lifts))
        def _():
            pl.semaphore_wait(barrier, replicas + 1)

    count = count_ref[0]
    scale = 1.0 / jnp.full((1, 1), count, jnp.int32).astype(F32)

    def block_rows(b):
        return pl.ds(pl.multiple_of(b * size, size), size)

    def normalise(b):
        here = block_rows(b)
        wide = acts[here, :].astype(F32)
        inv = lax.rsqrt(jnp.mean(wide * wide, axis=-1, keepdims=True) + EPSILON)
        unit_rows = wide * inv
        inv_rms[here, :] = jnp.broadcast_to(inv, (size, LANES))
        unit[here, :] = unit_rows
        normed[here, :] = (unit_rows * gain[...]).astype(BF16)

    def each_block(work):
        def body(b, carry):
            work(b)
            return carry

        lax.fori_loop(0, blocks, body, 0)

    def error_parts():
        p_part[:, :dw] = small_mm_nt(start_value[...], err_value[...])
        p_part[:, dw:] = small_mm_nt(start_out[...], err_out[...])

    def add_block(here):
        p_part[:, :dw] += small_mm(small_mm_nt(start_value[...], value_grad[here, :]) * scale, normed[here, :])
        p_part[:, dw:] += small_mm(small_mm_nt(start_out[...], grads[here, :]) * scale, values[here, :])

    def add_lower(here):
        along = small_mm_nt(lower_value_q[...], passed[here, :]) * scale
        lower_part[:, :dw] += small_mm(along, lower_normed[here, :])
        along = small_mm_nt(lower_out_q[...], passed[here, :]) * scale
        lower_part[:, dw:] += small_mm(along, lower_values[here, :])

    def lift(i):
        src, dst = [
            (normed, lower_normed),
            (values, lower_values),
            (value_q, lower_value_q),
            (start_out, lower_out_q),
            (p_part, lower_part),
        ][i]
        return pltpu.make_async_remote_copy(
            src_ref=src,
            dst_ref=dst,
            send_sem=lift_send.at[i],
            recv_sem=lift_recv.at[i],
            device_id={"section": lax.rem(section + 1, sections)},
            device_id_type=pl.DeviceIdType.MESH,
        )

    def piece(c):
        return slice(cuts[c], cuts[c + 1])

    def hop(b, c):
        return pltpu.make_async_remote_copy(
            src_ref=passed.at[block_rows(b), piece(c)],
            dst_ref=grads.at[block_rows(b), piece(c)],
            send_sem=relay_send.at[b * pieces + c],
            recv_sem=relay_recv.at[b * pieces + c],
            device_id={"section": lax.rem(section + last, sections)},
            device_id_type=pl.DeviceIdType.MESH,
        )

    def pass_on(b, mean, product):
        here = block_rows(b)
        inv = inv_rms[here, 0:1]
        for c in range(pieces):
            cols = piece(c)
            centred = product(cols) * gain[:, cols] - unit[here, cols] * mean
            passed[here, cols] = (grads[here, cols].astype(F32) + inv * centred).astype(BF16)
            if c + 1 == 2:
                for early in range(2):
                    hop(b, early).start()
        for c in range(2, pieces):
            hop(b, c).start()

    def project():
        wide = mm(normed[...], w_value[...])
        values_wide[...] = wide
        values[...] = wide.astype(BF16)
        normed_t[...] = normed[...].T

    @pl.when(section == last)
    def _():
        l_top.wait()
        live = lax.broadcasted_iota(jnp.int32, (rows, 1), 0) < count
        grads[...] = jnp.where(live, top[...].astype(F32), 0.0).astype(BF16)
        l_w_out.wait()
        value_grad[...] = mm_nt(grads[...], w_out[...]).astype(BF16)
        l_acts.wait()
        l_gain.wait()
        l_w_value.wait()
        for load in loads[5:]:
            load.start()
        norm_grad[...] = mm_nt(value_grad[...], w_value[...])
        all_here()

        def send(b):
            here = block_rows(b)
            normalise(b)
            mean = jnp.mean(norm_grad[here, :] * gain[...] * unit[here, :], axis=-1, keepdims=True)
            pass_on(b, mean, lambda cols: norm_grad[here, cols])

        each_block(send)
        project()
        for load in loads[5:]:
            load.wait()
        error_parts()

    @pl.when(section < last)
    def _():
        l_acts.wait()
        l_gain.wait()
        for load in loads[5:]:
            load.start()
        each_block(normalise)
        l_w_out.wait()
        w_out_t[...] = w_out[...].T
        l_w_value.wait()
        w_value_t[...] = w_value[...].T
        project()
        all_here()


        @pl.when(lifted)
        def _():
            lift(0).start()
            lift(1).start()

        for load in (l_top, *loads[5:]):
            load.wait()

        @pl.when(section < last - 1)
        def _():
            error_parts()

        @pl.when(lifted)
        def _():
            value_q[...] = small_mm(start_value[...], w_out[...])
            for i in range(2, 5):
                lift(i).start()

        def relay(b):
            here = block_rows(b)

            total = None
            for group in groups:
                for c in group:
                    hop(b, c).wait_recv()
                cols = slice(cuts[group[0]], cuts[group[-1] + 1])
                term = mm(grads[here, cols], w_out_t[cols, :])
                total = term if total is None else total + term
            v_rows = total.astype(BF16)
            value_grad[here, :] = v_rows

            @pl.when(section > 0)
            def _():
                mean = jnp.sum(v_rows.astype(F32) * values_wide[here, :], axis=-1, keepdims=True) * (1.0 / dw)
                pass_on(b, mean, lambda cols: mm(v_rows, w_value_t[:, cols]))

        each_block(relay)

        @pl.when(section == last - 1)
        def _():
            error_parts()

    def packed(x):
        return jnp.concatenate([x[:, :LANES], x[:, LANES:]], axis=0).astype(BF16)

    def arrivals(ref, amount, sem):
        return pltpu.make_async_copy(ref.at[pl.ds(0, amount)], ref.at[pl.ds(0, amount)], sem)

    side = math.isqrt(chips) if math.isqrt(chips) ** 2 == chips else 1
    height = chips // side

    def hops(offset):
        return min(offset[0], height - offset[0]) + min(offset[1], side - offset[1])

    offsets = sorted(((dy, dx) for dy in range(height) for dx in range(side)), key=hops, reverse=True)
    farthest_first = [
        (hops(o) == 0, lax.rem(chip // side + o[0], height) * side + lax.rem(lax.rem(chip, side) + o[1], side))
        for o in offsets
    ]

    def scatter(part, seen, phase, first, end):
        for here, to in farthest_first:

            wanted = (to >= first) & (to < end)

            @pl.when(wanted & (core == 0) if here else wanted)
            def _():
                pltpu.make_async_remote_copy(
                    src_ref=part.at[to],
                    dst_ref=seen.at[me],
                    send_sem=reduce_send.at[2 * phase],
                    recv_sem=reduce_recv.at[2 * phase],
                    device_id={"dp": 2 * to + 1},
                    device_id_type=pl.DeviceIdType.MESH,
                ).start()

    def summed(part, seen, phase):
        seen[me] = part[chip]
        arrivals(seen, replicas - 1, reduce_recv.at[2 * phase]).wait()
        return jnp.sum(seen[...].astype(F32), axis=0)

    def spread(source, total, phase, arrival, to_section, to_self):
        for here, to in farthest_first:
            for end in range(1 if here and not to_self else 2):
                pltpu.make_async_remote_copy(
                    src_ref=source.at[chip],
                    dst_ref=total.at[chip],
                    send_sem=reduce_send.at[2 * phase + 1],
                    recv_sem=reduce_recv.at[arrival],
                    device_id={"section": to_section, "dp": 2 * to + end},
                    device_id_type=pl.DeviceIdType.MESH,
                ).start()

    def gathered(total, phase):
        @pl.when(owner)
        def _():
            arrivals(total, tiles - 1, reduce_recv.at[2 * phase + 1]).wait()

        @pl.when(jnp.logical_not(owner))
        def _():
            arrivals(total, tiles, reduce_recv.at[2 * phase + 1]).wait()

    def pack_all(part, ref):
        for j in range(tiles):
            ref[j] = packed(part[:, 2 * LANES * j : 2 * LANES * (j + 1)])

    def finish_sends(seen, phase):
        @pl.when(owner)
        def _():
            arrivals(seen, tiles - 1, reduce_send.at[2 * phase]).wait()
            arrivals(seen, replicas - 1, reduce_send.at[2 * phase + 1]).wait()

        @pl.when(jnp.logical_not(owner))
        def _():
            arrivals(seen, tiles, reduce_send.at[2 * phase]).wait()

    @pl.when(lifts)
    def _():
        for i in range(5):
            lift(i).wait_recv()
        add_lower(slice(None))

        pack_all(lower_part, lower_packed)
        scatter(lower_packed, lower_seen, 2, 0, tiles)

    @pl.when(jnp.logical_not(lifted))
    def _():
        add_block(slice(None))
        pack_all(p_part, p_packed)
        scatter(p_packed, p_seen, 0, 0, tiles)

    @pl.when(lifts & owner)
    def _():
        lower_total[chip] = summed(lower_packed, lower_seen, 2).astype(BF16)
        spread(lower_total, p_total, 2, 1, section - 1, True)

    @pl.when(jnp.logical_not(lifted) & owner)
    def _():
        p_total[chip] = summed(p_packed, p_seen, 0).astype(BF16)
        spread(p_total, p_total, 0, 1, section, False)

    @pl.when(jnp.logical_not(lifted))
    def _():
        gathered(p_total, 0)

    @pl.when(lifted)
    def _():
        arrivals(p_total, tiles, reduce_recv.at[1]).wait()

    def unpacked(first, count):
        halves = [p_total[j] for j in range(first, first + count)]
        return jnp.concatenate([half for tile in halves for half in (tile[:8].astype(F32), tile[8:].astype(F32))], axis=1)

    p_value = unpacked(0, value_tiles)
    p_out = unpacked(value_tiles, out_tiles)
    p_all[:, :dw] = p_value
    p_all[:, dw:] = p_out
    p_value, p_out = p_value.astype(BF16), p_out.astype(BF16)
    q_out = small_mm(mm_nt(p_out, values[...]) * scale, grads[...]) + mm(p_out, err_out[...])
    for j in range(value_tiles):
        q_packed[out_tiles + j] = packed(q_out[:, 2 * LANES * j : 2 * LANES * (j + 1)])
    scatter(q_packed, q_seen, 1, out_tiles, tiles)
    q_value = small_mm(mm(p_value, normed_t[...]) * scale, value_grad[...]) + mm(p_value, err_value[...])
    for j in range(out_tiles):
        q_packed[j] = packed(q_value[:, 2 * LANES * j : 2 * LANES * (j + 1)])
    scatter(q_packed, q_seen, 1, 0, out_tiles)

    def factors():
        grams = [
            lax.dot_general(
                x, x, (((1,), (1,)), ((), ())), precision=lax.Precision.HIGHEST, preferred_element_type=F32
            )
            for x in (p_all[:, :dw], p_all[:, dw:])
        ]
        return [inverse_factor(gram) for gram in grams]

    def solved(pair, extra):
        for_value, for_out = extra
        lower = jnp.where(chip < out_tiles, for_value, for_out)
        return jnp.concatenate([apply_small(lower, pair[:8]), apply_small(lower, pair[8:])], axis=0)

    extra = factors()

    @pl.when(owner)
    def _():
        q_total[chip] = solved(summed(q_packed, q_seen, 1), extra).astype(BF16)
        spread(q_total, q_total, 1, 3, section, False)

    gathered(q_total, 1)
    for j in range(tiles):
        ref, place = (out_value, j) if j < out_tiles else (out_out, j - out_tiles)
        tile = q_total[j].astype(F32)
        ref[:, 2 * LANES * place : 2 * LANES * place + LANES] = tile[:8]
        ref[:, 2 * LANES * place + LANES : 2 * LANES * (place + 1)] = tile[8:]
    finish_sends(q_seen, 1)

    @pl.when(jnp.logical_not(lifted))
    def _():
        finish_sends(p_seen, 0)

    @pl.when(lifts)
    def _():
        @pl.when(owner)
        def _():
            arrivals(lower_seen, tiles - 1, reduce_send.at[4]).wait()
            arrivals(lower_seen, replicas, reduce_send.at[5]).wait()

        @pl.when(jnp.logical_not(owner))
        def _():
            arrivals(lower_seen, tiles, reduce_send.at[4]).wait()

    @pl.when(section > 0)
    def _():
        def sent(b):
            for c in range(pieces):
                hop(b, c).wait_send()

        each_block(sent)

    @pl.when(lifted)
    def _():
        for i in range(5):
            lift(i).wait_send()


def solution(mesh):
    sections, replicas = mesh.shape["section"], mesh.shape["dp"]

    def shards(
        acts, out_grad, tok_count, norm_gain, w_value, w_out, err_value, err_out, start_q_value, start_q_out
    ):
        rows, dw = out_grad.shape
        hv, rank = start_q_value.shape[1:]
        tiles = (dw + hv) // (2 * LANES)
        blocks = rows // 16
        cuts = tuple(cut * dw // CUTS[-1] for cut in CUTS)
        any_space = pl.BlockSpec(memory_space=pl.ANY)
        vmem = pl.BlockSpec(memory_space=pltpu.VMEM)
        q_value, q_out = pl.pallas_call(
            functools.partial(kernel, sections, replicas, blocks, cuts, GROUPS),
            out_shape=(pltpu.VMEM((rank, hv), F32), pltpu.VMEM((rank, dw), F32)),
            in_specs=[any_space] * 2 + [pl.BlockSpec(memory_space=pltpu.SMEM)] + [any_space] * 7,
            out_specs=(vmem, vmem),
            scratch_shapes=[
                pltpu.VMEM((rows, dw), BF16),
                pltpu.VMEM((rows, dw), BF16),
                pltpu.VMEM((1, dw), F32),
                pltpu.VMEM((dw, hv), BF16),
                pltpu.VMEM((hv, dw), BF16),
                pltpu.VMEM((dw, hv), BF16),
                pltpu.VMEM((hv, dw), BF16),
                pltpu.VMEM((rank, hv), F32),
                pltpu.VMEM((rank, dw), F32),
                pltpu.VMEM((hv, dw), BF16),
                pltpu.VMEM((dw, hv), BF16),
                pltpu.VMEM((rows, dw), F32),
                pltpu.VMEM((rows, LANES), F32),
                pltpu.VMEM((rows, dw), BF16),
                pltpu.VMEM((rows, hv), BF16),
                pltpu.VMEM((rows, hv), F32),
                pltpu.VMEM((rows, dw), BF16),
                pltpu.VMEM((rows, dw), BF16),
                pltpu.VMEM((rows, hv), BF16),
                pltpu.VMEM((rows, dw), F32),
                pltpu.VMEM((rank, dw + hv), F32),
                pltpu.VMEM((rank, dw + hv), F32),
                pltpu.VMEM((tiles, 2 * rank, LANES), BF16),
                pltpu.VMEM((tiles, 2 * rank, LANES), BF16),
                pltpu.VMEM((tiles, 2 * rank, LANES), BF16),
                pltpu.VMEM((tiles, 2 * rank, LANES), BF16),
                pltpu.VMEM((replicas, 2 * rank, LANES), BF16),
                pltpu.VMEM((replicas, 2 * rank, LANES), BF16),
                pltpu.SemaphoreType.DMA((9,)),
                pltpu.SemaphoreType.DMA((blocks * (len(cuts) - 1),)),
                pltpu.SemaphoreType.DMA((blocks * (len(cuts) - 1),)),
                pltpu.SemaphoreType.DMA((6,)),
                pltpu.SemaphoreType.DMA((6,)),
                pltpu.VMEM((rows, dw), BF16),
                pltpu.VMEM((rows, hv), BF16),
                pltpu.VMEM((rank, dw), F32),
                pltpu.VMEM((rank, dw), F32),
                pltpu.VMEM((rank, dw + hv), F32),
                pltpu.VMEM((tiles, 2 * rank, LANES), BF16),
                pltpu.VMEM((replicas, 2 * rank, LANES), BF16),
                pltpu.VMEM((tiles, 2 * rank, LANES), BF16),
                pltpu.VMEM((rank, dw), F32),
                pltpu.VMEM((dw, rows), BF16),
                pltpu.SemaphoreType.DMA((5,)),
                pltpu.SemaphoreType.DMA((5,)),
            ],
            compiler_params=pltpu.CompilerParams(
                collective_id=0, has_side_effects=True, vmem_limit_bytes=60 * 2**20
            ),
            cost_estimate=pl.CostEstimate(flops=1_700_000_000, bytes_accessed=12_000_000, transcendentals=0),
        )(
            acts[0],
            out_grad,
            tok_count,
            norm_gain,
            w_value[0],
            w_out[0],
            err_value[0],
            err_out[0],
            start_q_value[0].T,
            start_q_out[0].T,
        )
        return q_value.T[None], q_out.T[None]

    placed = (
        P("section", "dp", None),
        P("dp", None),
        P("dp"),
        P("section", None),
        P("section", None, None),
        P("section", None, None),
        P("section", "dp", None),
        P("section", "dp", None),
        P("section", None, None),
        P("section", None, None),
    )
    return jax.shard_map(
        shards,
        mesh=mesh,
        in_specs=placed,
        out_specs=(P("section", None, None), P("section", None, None)),
        check_vma=False,
    )
```

```python
import functools
import math

import jax
import jax.numpy as jnp
from jax import lax
from jax.experimental import pallas as pl
from jax.experimental.pallas import tpu as pltpu
from jax.sharding import PartitionSpec as P

EPSILON = 1e-06
LANES = 128
CUTS = (0, 5, 10, 15, 20)
GROUPS = ((0,), (1,), (2,), (3,))
LIFTED = 2
BF16 = jnp.bfloat16
F32 = jnp.float32


def mm(a, b):
    return lax.dot_general(a, b, (((1,), (0,)), ((), ())), preferred_element_type=F32)


def mm_nt(a, b):
    return lax.dot_general(a, b, (((1,), (1,)), ((), ())), preferred_element_type=F32)


def split(x):
    high = x.astype(BF16).astype(F32)
    return jnp.concatenate([high, x - high], axis=0).astype(BF16)


def joined(product):
    half = product.shape[0] // 2
    return product[:half] + product[half:]


def small_mm(x, big):
    return joined(mm(split(x), big))


def small_mm_nt(x, big):
    return joined(mm_nt(split(x), big))


def inverse_factor(gram):
    n = gram.shape[0]
    row = lax.broadcasted_iota(jnp.int32, (n, n), 0)
    col = lax.broadcasted_iota(jnp.int32, (n, n), 1)
    work = jnp.concatenate([gram, jnp.where(row == col, 1.0, 0.0)], axis=1)
    line = lax.broadcasted_iota(jnp.int32, (n, 2 * n), 0)
    for k in range(n):
        root = lax.rsqrt(work[k : k + 1, k : k + 1])
        pivot = work[k : k + 1, :] * root
        factor = work[:, k : k + 1] * root
        work = jnp.where(line == k, pivot, jnp.where(line > k, work - factor * pivot, work))
    return work[:, n:]


def apply_small(lower, tile):
    total = lower[:, 0:1] * tile[0:1, :]
    for k in range(1, lower.shape[1]):
        total = total + lower[:, k : k + 1] * tile[k : k + 1, :]
    return total


def kernel(
    sections,
    replicas,
    blocks,
    cuts,
    groups,
    acts_hbm,
    top_hbm,
    count_ref,
    gain_hbm,
    w_value_hbm,
    w_out_hbm,
    err_value_hbm,
    err_out_hbm,
    q_value_hbm,
    q_out_hbm,
    out_value,
    out_out,
    acts,
    top,
    gain,
    w_value,
    w_out,
    err_value,
    err_out,
    start_value,
    start_out,
    w_value_t,
    w_out_t,
    unit,
    inv_rms,
    normed,
    values,
    values_wide,
    grads,
    passed,
    value_grad,
    norm_grad,
    p_part,
    p_all,
    p_packed,
    q_packed,
    p_total,
    q_total,
    p_seen,
    q_seen,
    load_sem,
    relay_send,
    relay_recv,
    reduce_send,
    reduce_recv,
    lower_normed,
    lower_values,
    lower_value_q,
    lower_out_q,
    lower_part,
    lower_packed,
    lower_seen,
    lower_total,
    value_q,
    normed_t,
    lift_send,
    lift_recv,
):
    section = lax.axis_index("section")
    me = lax.axis_index("dp")
    rows, dw = acts.shape
    hv = w_out.shape[0]
    size = rows // blocks
    value_tiles, out_tiles = dw // (2 * LANES), hv // (2 * LANES)
    tiles = value_tiles + out_tiles
    last = sections - 1
    chips = replicas // 2
    chip, core = me // 2, lax.rem(me, 2)
    owner = (core == 1) & (chip < tiles)
    lifted = section < LIFTED
    lifts = (section > 0) & (section <= LIFTED)
    pieces = len(cuts) - 1

    loads = [
        pltpu.make_async_copy(src, dst, load_sem.at[i])
        for i, (src, dst) in enumerate(
            [
                (top_hbm, top),
                (w_out_hbm, w_out),
                (acts_hbm, acts),
                (gain_hbm, gain),
                (w_value_hbm, w_value),
                (q_value_hbm, start_value),
                (q_out_hbm, start_out),
                (err_value_hbm, err_value),
                (err_out_hbm, err_out),
            ]
        )
    ]
    (l_top, l_w_out, l_acts, l_gain, l_w_value, l_q_value, l_q_out, l_err_value, l_err_out) = loads
    for load in loads[:5]:
        load.start()

    barrier = pltpu.get_barrier_semaphore()

    def greet(k, carry):
        pl.semaphore_signal(
            barrier, inc=1, device_id={"dp": lax.rem(me + k, replicas)}, device_id_type=pl.DeviceIdType.MESH
        )
        return carry

    for step in (1, sections - 1):
        pl.semaphore_signal(
            barrier,
            inc=1,
            device_id={"section": lax.rem(section + step, sections)},
            device_id_type=pl.DeviceIdType.MESH,
        )
    lax.fori_loop(1, replicas, greet, 0)

    @pl.when(lifted)
    def _():
        def greet_owner(k, carry):
            pl.semaphore_signal(
                barrier,
                inc=1,
                device_id={"section": section + 1, "dp": 2 * k + 1},
                device_id_type=pl.DeviceIdType.MESH,
            )
            return carry

        lax.fori_loop(0, tiles, greet_owner, 0)

    def all_here():
        @pl.when(owner & lifts)
        def _():
            pl.semaphore_wait(barrier, 2 * replicas + 1)

        @pl.when(jnp.logical_not(owner & lifts))
        def _():
            pl.semaphore_wait(barrier, replicas + 1)

    count = count_ref[0]
    scale = 1.0 / jnp.full((1, 1), count, jnp.int32).astype(F32)

    def block_rows(b):
        return pl.ds(pl.multiple_of(b * size, size), size)

    def normalise(b):
        here = block_rows(b)
        wide = acts[here, :].astype(F32)
        inv = lax.rsqrt(jnp.mean(wide * wide, axis=-1, keepdims=True) + EPSILON)
        unit_rows = wide * inv
        inv_rms[here, :] = jnp.broadcast_to(inv, (size, LANES))
        unit[here, :] = unit_rows
        normed[here, :] = (unit_rows * gain[...]).astype(BF16)

    def each_block(work):
        def body(b, carry):
            work(b)
            return carry

        lax.fori_loop(0, blocks, body, 0)

    def error_parts():
        p_part[:, :dw] = small_mm_nt(start_value[...], err_value[...])
        p_part[:, dw:] = small_mm_nt(start_out[...], err_out[...])

    def add_block(here):
        p_part[:, :dw] += small_mm(small_mm_nt(start_value[...], value_grad[here, :]) * scale, normed[here, :])
        p_part[:, dw:] += small_mm(small_mm_nt(start_out[...], grads[here, :]) * scale, values[here, :])

    def pack_some(part, ref, first, end):
        for j in range(first, end):
            ref[j] = packed(part[:, 2 * LANES * j : 2 * LANES * (j + 1)])

    def lower_sums():
        factors_below = jnp.concatenate([lower_value_q[...], lower_out_q[...]], axis=0)
        along = small_mm_nt(factors_below, passed[...]) * scale
        rank = lower_part.shape[0]
        lower_part[:, :dw] += small_mm(along[:rank], lower_normed[...])
        pack_some(lower_part, lower_packed, 0, value_tiles)
        scatter(lower_packed, lower_seen, 2, 0, value_tiles)
        lower_part[:, dw:] += small_mm(along[rank:], lower_values[...])
        pack_some(lower_part, lower_packed, value_tiles, tiles)
        scatter(lower_packed, lower_seen, 2, value_tiles, tiles)

    def lift(i):
        src, dst = [
            (normed, lower_normed),
            (values, lower_values),
            (value_q, lower_value_q),
            (start_out, lower_out_q),
            (p_part, lower_part),
        ][i]
        return pltpu.make_async_remote_copy(
            src_ref=src,
            dst_ref=dst,
            send_sem=lift_send.at[i],
            recv_sem=lift_recv.at[i],
            device_id={"section": lax.rem(section + 1, sections)},
            device_id_type=pl.DeviceIdType.MESH,
        )

    def piece(c):
        return slice(cuts[c], cuts[c + 1])

    def hop(b, c):
        return pltpu.make_async_remote_copy(
            src_ref=passed.at[block_rows(b), piece(c)],
            dst_ref=grads.at[block_rows(b), piece(c)],
            send_sem=relay_send.at[b * pieces + c],
            recv_sem=relay_recv.at[b * pieces + c],
            device_id={"section": lax.rem(section + last, sections)},
            device_id_type=pl.DeviceIdType.MESH,
        )

    def pass_on(b, mean, product):
        here = block_rows(b)
        inv = inv_rms[here, 0:1]
        for c in range(pieces):
            cols = piece(c)
            centred = product(cols) * gain[:, cols] - unit[here, cols] * mean
            passed[here, cols] = (grads[here, cols].astype(F32) + inv * centred).astype(BF16)
            if c + 1 == 2:
                for early in range(2):
                    hop(b, early).start()
        for c in range(2, pieces):
            hop(b, c).start()

    def project():
        wide = mm(normed[...], w_value[...])
        values_wide[...] = wide
        values[...] = wide.astype(BF16)
        normed_t[...] = normed[...].T

    @pl.when(section == last)
    def _():
        l_top.wait()
        live = lax.broadcasted_iota(jnp.int32, (rows, 1), 0) < count
        grads[...] = jnp.where(live, top[...].astype(F32), 0.0).astype(BF16)
        l_w_out.wait()
        value_grad[...] = mm_nt(grads[...], w_out[...]).astype(BF16)
        l_acts.wait()
        l_gain.wait()
        l_w_value.wait()
        for load in loads[5:]:
            load.start()
        norm_grad[...] = mm_nt(value_grad[...], w_value[...])
        all_here()

        def send(b):
            here = block_rows(b)
            normalise(b)
            mean = jnp.mean(norm_grad[here, :] * gain[...] * unit[here, :], axis=-1, keepdims=True)
            pass_on(b, mean, lambda cols: norm_grad[here, cols])

        each_block(send)
        project()
        for load in loads[5:]:
            load.wait()
        error_parts()

    @pl.when(section < last)
    def _():
        l_acts.wait()
        l_gain.wait()
        for load in loads[5:]:
            load.start()
        each_block(normalise)
        l_w_out.wait()
        w_out_t[...] = w_out[...].T
        l_w_value.wait()
        w_value_t[...] = w_value[...].T
        project()
        all_here()


        @pl.when(lifted)
        def _():
            lift(0).start()
            lift(1).start()

        for load in (l_top, *loads[5:]):
            load.wait()

        @pl.when(section < last - 1)
        def _():
            error_parts()

        @pl.when(lifted)
        def _():
            value_q[...] = small_mm(start_value[...], w_out[...])
            for i in range(2, 5):
                lift(i).start()

        def relay(b):
            here = block_rows(b)

            total = None
            for group in groups:
                for c in group:
                    hop(b, c).wait_recv()
                cols = slice(cuts[group[0]], cuts[group[-1] + 1])
                term = mm(grads[here, cols], w_out_t[cols, :])
                total = term if total is None else total + term
            v_rows = total.astype(BF16)
            value_grad[here, :] = v_rows

            @pl.when(section > 0)
            def _():
                mean = jnp.sum(v_rows.astype(F32) * values_wide[here, :], axis=-1, keepdims=True) * (1.0 / dw)
                pass_on(b, mean, lambda cols: mm(v_rows, w_value_t[:, cols]))

        each_block(relay)

        @pl.when(section == last - 1)
        def _():
            error_parts()

    def packed(x):
        return jnp.concatenate([x[:, :LANES], x[:, LANES:]], axis=0).astype(BF16)

    def arrivals(ref, amount, sem):
        return pltpu.make_async_copy(ref.at[pl.ds(0, amount)], ref.at[pl.ds(0, amount)], sem)

    side = math.isqrt(chips) if math.isqrt(chips) ** 2 == chips else 1
    height = chips // side

    def hops(offset):
        return min(offset[0], height - offset[0]) + min(offset[1], side - offset[1])

    offsets = sorted(((dy, dx) for dy in range(height) for dx in range(side)), key=hops, reverse=True)
    farthest_first = [
        (hops(o) == 0, lax.rem(chip // side + o[0], height) * side + lax.rem(lax.rem(chip, side) + o[1], side))
        for o in offsets
    ]

    def scatter(part, seen, phase, first, end):
        for here, to in farthest_first:

            wanted = (to >= first) & (to < end)

            @pl.when(wanted & (core == 0) if here else wanted)
            def _():
                pltpu.make_async_remote_copy(
                    src_ref=part.at[to],
                    dst_ref=seen.at[me],
                    send_sem=reduce_send.at[2 * phase],
                    recv_sem=reduce_recv.at[2 * phase],
                    device_id={"dp": 2 * to + 1},
                    device_id_type=pl.DeviceIdType.MESH,
                ).start()

    def summed(part, seen, phase):
        seen[me] = part[chip]
        arrivals(seen, replicas - 1, reduce_recv.at[2 * phase]).wait()
        return jnp.sum(seen[...].astype(F32), axis=0)

    def spread(source, total, phase, arrival, to_section, to_self):
        for here, to in farthest_first:
            for end in range(1 if here and not to_self else 2):
                pltpu.make_async_remote_copy(
                    src_ref=source.at[chip],
                    dst_ref=total.at[chip],
                    send_sem=reduce_send.at[2 * phase + 1],
                    recv_sem=reduce_recv.at[arrival],
                    device_id={"section": to_section, "dp": 2 * to + end},
                    device_id_type=pl.DeviceIdType.MESH,
                ).start()

    def gathered(total, phase):
        @pl.when(owner)
        def _():
            arrivals(total, tiles - 1, reduce_recv.at[2 * phase + 1]).wait()

        @pl.when(jnp.logical_not(owner))
        def _():
            arrivals(total, tiles, reduce_recv.at[2 * phase + 1]).wait()

    def finish_sends(seen, phase):
        @pl.when(owner)
        def _():
            arrivals(seen, tiles - 1, reduce_send.at[2 * phase]).wait()
            arrivals(seen, replicas - 1, reduce_send.at[2 * phase + 1]).wait()

        @pl.when(jnp.logical_not(owner))
        def _():
            arrivals(seen, tiles, reduce_send.at[2 * phase]).wait()

    @pl.when(lifts)
    def _():
        for i in range(5):
            lift(i).wait_recv()
        lower_sums()


    @pl.when(jnp.logical_not(lifted))
    def _():
        add_block(slice(None))
        pack_some(p_part, p_packed, 0, tiles)
        scatter(p_packed, p_seen, 0, 0, tiles)

    @pl.when(lifts & owner)
    def _():
        lower_total[chip] = summed(lower_packed, lower_seen, 2).astype(BF16)
        spread(lower_total, p_total, 2, 1, section - 1, True)

    @pl.when(jnp.logical_not(lifted) & owner)
    def _():
        p_total[chip] = summed(p_packed, p_seen, 0).astype(BF16)
        spread(p_total, p_total, 0, 1, section, False)

    @pl.when(jnp.logical_not(lifted))
    def _():
        gathered(p_total, 0)

    @pl.when(lifted)
    def _():
        arrivals(p_total, tiles, reduce_recv.at[1]).wait()

    def unpacked(first, count):
        halves = [p_total[j] for j in range(first, first + count)]
        return jnp.concatenate([half for tile in halves for half in (tile[:8].astype(F32), tile[8:].astype(F32))], axis=1)

    p_value = unpacked(0, value_tiles)
    p_out = unpacked(value_tiles, out_tiles)
    p_all[:, :dw] = p_value
    p_all[:, dw:] = p_out
    p_value, p_out = p_value.astype(BF16), p_out.astype(BF16)
    q_out = small_mm(mm_nt(p_out, values[...]) * scale, grads[...]) + mm(p_out, err_out[...])
    for j in range(value_tiles):
        q_packed[out_tiles + j] = packed(q_out[:, 2 * LANES * j : 2 * LANES * (j + 1)])
    scatter(q_packed, q_seen, 1, out_tiles, tiles)
    q_value = small_mm(mm(p_value, normed_t[...]) * scale, value_grad[...]) + mm(p_value, err_value[...])
    for j in range(out_tiles):
        q_packed[j] = packed(q_value[:, 2 * LANES * j : 2 * LANES * (j + 1)])
    scatter(q_packed, q_seen, 1, 0, out_tiles)

    def factors():
        grams = [
            lax.dot_general(
                x, x, (((1,), (1,)), ((), ())), precision=lax.Precision.HIGHEST, preferred_element_type=F32
            )
            for x in (p_all[:, :dw], p_all[:, dw:])
        ]
        return [inverse_factor(gram) for gram in grams]

    def solved(pair, extra):
        for_value, for_out = extra
        lower = jnp.where(chip < out_tiles, for_value, for_out)
        return jnp.concatenate([apply_small(lower, pair[:8]), apply_small(lower, pair[8:])], axis=0)

    extra = factors()

    @pl.when(owner)
    def _():
        q_total[chip] = solved(summed(q_packed, q_seen, 1), extra).astype(BF16)
        spread(q_total, q_total, 1, 3, section, False)

    gathered(q_total, 1)
    for j in range(tiles):
        ref, place = (out_value, j) if j < out_tiles else (out_out, j - out_tiles)
        tile = q_total[j].astype(F32)
        ref[:, 2 * LANES * place : 2 * LANES * place + LANES] = tile[:8]
        ref[:, 2 * LANES * place + LANES : 2 * LANES * (place + 1)] = tile[8:]
    finish_sends(q_seen, 1)

    @pl.when(jnp.logical_not(lifted))
    def _():
        finish_sends(p_seen, 0)

    @pl.when(lifts)
    def _():
        @pl.when(owner)
        def _():
            arrivals(lower_seen, tiles - 1, reduce_send.at[4]).wait()
            arrivals(lower_seen, replicas, reduce_send.at[5]).wait()

        @pl.when(jnp.logical_not(owner))
        def _():
            arrivals(lower_seen, tiles, reduce_send.at[4]).wait()

    @pl.when(section > 0)
    def _():
        def sent(b):
            for c in range(pieces):
                hop(b, c).wait_send()

        each_block(sent)

    @pl.when(lifted)
    def _():
        for i in range(5):
            lift(i).wait_send()


def solution(mesh):
    sections, replicas = mesh.shape["section"], mesh.shape["dp"]

    def shards(
        acts, out_grad, tok_count, norm_gain, w_value, w_out, err_value, err_out, start_q_value, start_q_out
    ):
        rows, dw = out_grad.shape
        hv, rank = start_q_value.shape[1:]
        tiles = (dw + hv) // (2 * LANES)
        blocks = rows // 16
        cuts = tuple(cut * dw // CUTS[-1] for cut in CUTS)
        any_space = pl.BlockSpec(memory_space=pl.ANY)
        vmem = pl.BlockSpec(memory_space=pltpu.VMEM)
        q_value, q_out = pl.pallas_call(
            functools.partial(kernel, sections, replicas, blocks, cuts, GROUPS),
            out_shape=(pltpu.VMEM((rank, hv), F32), pltpu.VMEM((rank, dw), F32)),
            in_specs=[any_space] * 2 + [pl.BlockSpec(memory_space=pltpu.SMEM)] + [any_space] * 7,
            out_specs=(vmem, vmem),
            scratch_shapes=[
                pltpu.VMEM((rows, dw), BF16),
                pltpu.VMEM((rows, dw), BF16),
                pltpu.VMEM((1, dw), F32),
                pltpu.VMEM((dw, hv), BF16),
                pltpu.VMEM((hv, dw), BF16),
                pltpu.VMEM((dw, hv), BF16),
                pltpu.VMEM((hv, dw), BF16),
                pltpu.VMEM((rank, hv), F32),
                pltpu.VMEM((rank, dw), F32),
                pltpu.VMEM((hv, dw), BF16),
                pltpu.VMEM((dw, hv), BF16),
                pltpu.VMEM((rows, dw), F32),
                pltpu.VMEM((rows, LANES), F32),
                pltpu.VMEM((rows, dw), BF16),
                pltpu.VMEM((rows, hv), BF16),
                pltpu.VMEM((rows, hv), F32),
                pltpu.VMEM((rows, dw), BF16),
                pltpu.VMEM((rows, dw), BF16),
                pltpu.VMEM((rows, hv), BF16),
                pltpu.VMEM((rows, dw), F32),
                pltpu.VMEM((rank, dw + hv), F32),
                pltpu.VMEM((rank, dw + hv), F32),
                pltpu.VMEM((tiles, 2 * rank, LANES), BF16),
                pltpu.VMEM((tiles, 2 * rank, LANES), BF16),
                pltpu.VMEM((tiles, 2 * rank, LANES), BF16),
                pltpu.VMEM((tiles, 2 * rank, LANES), BF16),
                pltpu.VMEM((replicas, 2 * rank, LANES), BF16),
                pltpu.VMEM((replicas, 2 * rank, LANES), BF16),
                pltpu.SemaphoreType.DMA((9,)),
                pltpu.SemaphoreType.DMA((blocks * (len(cuts) - 1),)),
                pltpu.SemaphoreType.DMA((blocks * (len(cuts) - 1),)),
                pltpu.SemaphoreType.DMA((6,)),
                pltpu.SemaphoreType.DMA((6,)),
                pltpu.VMEM((rows, dw), BF16),
                pltpu.VMEM((rows, hv), BF16),
                pltpu.VMEM((rank, dw), F32),
                pltpu.VMEM((rank, dw), F32),
                pltpu.VMEM((rank, dw + hv), F32),
                pltpu.VMEM((tiles, 2 * rank, LANES), BF16),
                pltpu.VMEM((replicas, 2 * rank, LANES), BF16),
                pltpu.VMEM((tiles, 2 * rank, LANES), BF16),
                pltpu.VMEM((rank, dw), F32),
                pltpu.VMEM((dw, rows), BF16),
                pltpu.SemaphoreType.DMA((5,)),
                pltpu.SemaphoreType.DMA((5,)),
            ],
            compiler_params=pltpu.CompilerParams(
                collective_id=0, has_side_effects=True, vmem_limit_bytes=60 * 2**20
            ),
            cost_estimate=pl.CostEstimate(flops=1_700_000_000, bytes_accessed=12_000_000, transcendentals=0),
        )(
            acts[0],
            out_grad,
            tok_count,
            norm_gain,
            w_value[0],
            w_out[0],
            err_value[0],
            err_out[0],
            start_q_value[0].T,
            start_q_out[0].T,
        )
        return q_value.T[None], q_out.T[None]

    placed = (
        P("section", "dp", None),
        P("dp", None),
        P("dp"),
        P("section", None),
        P("section", None, None),
        P("section", None, None),
        P("section", "dp", None),
        P("section", "dp", None),
        P("section", None, None),
        P("section", None, None),
    )
    return jax.shard_map(
        shards,
        mesh=mesh,
        in_specs=placed,
        out_specs=(P("section", None, None), P("section", None, None)),
        check_vma=False,
    )
```

```python
import functools
import math

import jax
import jax.numpy as jnp
from jax import lax
from jax.experimental import pallas as pl
from jax.experimental.pallas import tpu as pltpu
from jax.sharding import PartitionSpec as P

EPSILON = 1e-06
LANES = 128
CUTS = (0, 6, 12, 17, 20)
GROUPS = ((0,), (1,), (2,), (3,))
LIFTED = 2
BF16 = jnp.bfloat16
F32 = jnp.float32


def mm(a, b):
    return lax.dot_general(a, b, (((1,), (0,)), ((), ())), preferred_element_type=F32)


def mm_nt(a, b):
    return lax.dot_general(a, b, (((1,), (1,)), ((), ())), preferred_element_type=F32)


def split(x):
    high = x.astype(BF16).astype(F32)
    return jnp.concatenate([high, x - high], axis=0).astype(BF16)


def joined(product):
    half = product.shape[0] // 2
    return product[:half] + product[half:]


def small_mm(x, big):
    return joined(mm(split(x), big))


def small_mm_nt(x, big):
    return joined(mm_nt(split(x), big))


def inverse_factor(gram):
    n = gram.shape[0]
    row = lax.broadcasted_iota(jnp.int32, (n, n), 0)
    col = lax.broadcasted_iota(jnp.int32, (n, n), 1)
    work = jnp.concatenate([gram, jnp.where(row == col, 1.0, 0.0)], axis=1)
    line = lax.broadcasted_iota(jnp.int32, (n, 2 * n), 0)
    for k in range(n):
        root = lax.rsqrt(work[k : k + 1, k : k + 1])
        pivot = work[k : k + 1, :] * root
        factor = work[:, k : k + 1] * root
        work = jnp.where(line == k, pivot, jnp.where(line > k, work - factor * pivot, work))
    return work[:, n:]


def apply_small(lower, tile):
    total = lower[:, 0:1] * tile[0:1, :]
    for k in range(1, lower.shape[1]):
        total = total + lower[:, k : k + 1] * tile[k : k + 1, :]
    return total


def kernel(
    sections,
    replicas,
    blocks,
    cuts,
    groups,
    acts_hbm,
    top_hbm,
    count_ref,
    gain_hbm,
    w_value_hbm,
    w_out_hbm,
    err_value_hbm,
    err_out_hbm,
    q_value_hbm,
    q_out_hbm,
    out_value,
    out_out,
    acts,
    top,
    gain,
    w_value,
    w_out,
    err_value,
    err_out,
    start_value,
    start_out,
    w_value_t,
    w_out_t,
    unit,
    inv_rms,
    normed,
    values,
    values_wide,
    grads,
    passed,
    value_grad,
    norm_grad,
    p_part,
    p_all,
    p_packed,
    q_packed,
    p_total,
    q_total,
    p_seen,
    q_seen,
    load_sem,
    relay_send,
    relay_recv,
    reduce_send,
    reduce_recv,
    lower_normed,
    lower_values,
    lower_value_q,
    lower_out_q,
    lower_part,
    lower_packed,
    lower_seen,
    lower_total,
    value_q,
    normed_t,
    lift_send,
    lift_recv,
):
    section = lax.axis_index("section")
    me = lax.axis_index("dp")
    rows, dw = acts.shape
    hv = w_out.shape[0]
    size = rows // blocks
    value_tiles, out_tiles = dw // (2 * LANES), hv // (2 * LANES)
    tiles = value_tiles + out_tiles
    last = sections - 1
    chips = replicas // 2
    chip, core = me // 2, lax.rem(me, 2)
    owner = (core == 1) & (chip < tiles)
    lifted = section < LIFTED
    lifts = (section > 0) & (section <= LIFTED)
    pieces = len(cuts) - 1

    loads = [
        pltpu.make_async_copy(src, dst, load_sem.at[i])
        for i, (src, dst) in enumerate(
            [
                (top_hbm, top),
                (w_out_hbm, w_out),
                (acts_hbm, acts),
                (gain_hbm, gain),
                (w_value_hbm, w_value),
                (q_value_hbm, start_value),
                (q_out_hbm, start_out),
                (err_value_hbm, err_value),
                (err_out_hbm, err_out),
            ]
        )
    ]
    (l_top, l_w_out, l_acts, l_gain, l_w_value, l_q_value, l_q_out, l_err_value, l_err_out) = loads
    for load in loads[:5]:
        load.start()

    barrier = pltpu.get_barrier_semaphore()

    def greet(k, carry):
        pl.semaphore_signal(
            barrier, inc=1, device_id={"dp": lax.rem(me + k, replicas)}, device_id_type=pl.DeviceIdType.MESH
        )
        return carry

    for step in (1, sections - 1):
        pl.semaphore_signal(
            barrier,
            inc=1,
            device_id={"section": lax.rem(section + step, sections)},
            device_id_type=pl.DeviceIdType.MESH,
        )
    lax.fori_loop(1, replicas, greet, 0)

    @pl.when(lifted)
    def _():
        def greet_owner(k, carry):
            pl.semaphore_signal(
                barrier,
                inc=1,
                device_id={"section": section + 1, "dp": 2 * k + 1},
                device_id_type=pl.DeviceIdType.MESH,
            )
            return carry

        lax.fori_loop(0, tiles, greet_owner, 0)

    def all_here():
        @pl.when(owner & lifts)
        def _():
            pl.semaphore_wait(barrier, 2 * replicas + 1)

        @pl.when(jnp.logical_not(owner & lifts))
        def _():
            pl.semaphore_wait(barrier, replicas + 1)

    count = count_ref[0]
    scale = 1.0 / jnp.full((1, 1), count, jnp.int32).astype(F32)

    def block_rows(b):
        return pl.ds(pl.multiple_of(b * size, size), size)

    def normalise(b):
        here = block_rows(b)
        wide = acts[here, :].astype(F32)
        inv = lax.rsqrt(jnp.mean(wide * wide, axis=-1, keepdims=True) + EPSILON)
        unit_rows = wide * inv
        inv_rms[here, :] = jnp.broadcast_to(inv, (size, LANES))
        unit[here, :] = unit_rows
        normed[here, :] = (unit_rows * gain[...]).astype(BF16)

    def each_block(work):
        def body(b, carry):
            work(b)
            return carry

        lax.fori_loop(0, blocks, body, 0)

    def error_parts():
        p_part[:, :dw] = small_mm_nt(start_value[...], err_value[...])
        p_part[:, dw:] = small_mm_nt(start_out[...], err_out[...])

    def add_block(here):
        p_part[:, :dw] += small_mm(small_mm_nt(start_value[...], value_grad[here, :]) * scale, normed[here, :])
        p_part[:, dw:] += small_mm(small_mm_nt(start_out[...], grads[here, :]) * scale, values[here, :])

    def pack_some(part, ref, first, end):
        for j in range(first, end):
            ref[j] = packed(part[:, 2 * LANES * j : 2 * LANES * (j + 1)])

    def lower_sums():
        factors_below = jnp.concatenate([lower_value_q[...], lower_out_q[...]], axis=0)
        along = small_mm_nt(factors_below, passed[...]) * scale
        rank = lower_part.shape[0]
        lower_part[:, :dw] += small_mm(along[:rank], lower_normed[...])
        pack_some(lower_part, lower_packed, 0, value_tiles)
        scatter(lower_packed, lower_seen, 2, 0, value_tiles)
        lower_part[:, dw:] += small_mm(along[rank:], lower_values[...])
        pack_some(lower_part, lower_packed, value_tiles, tiles)
        scatter(lower_packed, lower_seen, 2, value_tiles, tiles)

    def lift(i):
        src, dst = [
            (normed, lower_normed),
            (values, lower_values),
            (value_q, lower_value_q),
            (start_out, lower_out_q),
            (p_part, lower_part),
        ][i]
        return pltpu.make_async_remote_copy(
            src_ref=src,
            dst_ref=dst,
            send_sem=lift_send.at[i],
            recv_sem=lift_recv.at[i],
            device_id={"section": lax.rem(section + 1, sections)},
            device_id_type=pl.DeviceIdType.MESH,
        )

    def piece(c):
        return slice(cuts[c], cuts[c + 1])

    def hop(b, c):
        return pltpu.make_async_remote_copy(
            src_ref=passed.at[block_rows(b), piece(c)],
            dst_ref=grads.at[block_rows(b), piece(c)],
            send_sem=relay_send.at[b * pieces + c],
            recv_sem=relay_recv.at[b * pieces + c],
            device_id={"section": lax.rem(section + last, sections)},
            device_id_type=pl.DeviceIdType.MESH,
        )

    def pass_on(b, mean, product):
        here = block_rows(b)
        inv = inv_rms[here, 0:1]
        for c in range(pieces):
            cols = piece(c)
            centred = product(cols) * gain[:, cols] - unit[here, cols] * mean
            passed[here, cols] = (grads[here, cols].astype(F32) + inv * centred).astype(BF16)
            if c + 1 == 2:
                for early in range(2):
                    hop(b, early).start()
        for c in range(2, pieces):
            hop(b, c).start()

    def project():
        wide = mm(normed[...], w_value[...])
        values_wide[...] = wide
        values[...] = wide.astype(BF16)
        normed_t[...] = normed[...].T

    @pl.when(section == last)
    def _():
        l_top.wait()
        live = lax.broadcasted_iota(jnp.int32, (rows, 1), 0) < count
        grads[...] = jnp.where(live, top[...].astype(F32), 0.0).astype(BF16)
        l_w_out.wait()
        value_grad[...] = mm_nt(grads[...], w_out[...]).astype(BF16)
        l_acts.wait()
        l_gain.wait()
        l_w_value.wait()
        for load in loads[5:]:
            load.start()
        norm_grad[...] = mm_nt(value_grad[...], w_value[...])
        all_here()

        def send(b):
            here = block_rows(b)
            normalise(b)
            mean = jnp.mean(norm_grad[here, :] * gain[...] * unit[here, :], axis=-1, keepdims=True)
            pass_on(b, mean, lambda cols: norm_grad[here, cols])

        each_block(send)
        project()
        for load in loads[5:]:
            load.wait()
        error_parts()

    @pl.when(section < last)
    def _():
        l_acts.wait()
        l_gain.wait()
        for load in loads[5:]:
            load.start()
        each_block(normalise)
        l_w_out.wait()
        w_out_t[...] = w_out[...].T
        l_w_value.wait()
        w_value_t[...] = w_value[...].T
        project()
        all_here()


        @pl.when(lifted)
        def _():
            lift(0).start()
            lift(1).start()

        for load in (l_top, *loads[5:]):
            load.wait()

        @pl.when(section < last - 1)
        def _():
            error_parts()

        @pl.when(lifted)
        def _():
            value_q[...] = small_mm(start_value[...], w_out[...])
            for i in range(2, 5):
                lift(i).start()

        def relay(b):
            here = block_rows(b)

            total = None
            for group in groups:
                for c in group:
                    hop(b, c).wait_recv()
                cols = slice(cuts[group[0]], cuts[group[-1] + 1])
                term = mm(grads[here, cols], w_out_t[cols, :])
                total = term if total is None else total + term
            v_rows = total.astype(BF16)
            value_grad[here, :] = v_rows

            @pl.when(section > 0)
            def _():
                mean = jnp.sum(v_rows.astype(F32) * values_wide[here, :], axis=-1, keepdims=True) * (1.0 / dw)
                pass_on(b, mean, lambda cols: mm(v_rows, w_value_t[:, cols]))

        each_block(relay)

        @pl.when(section == last - 1)
        def _():
            error_parts()

    def packed(x):
        return jnp.concatenate([x[:, :LANES], x[:, LANES:]], axis=0).astype(BF16)

    def arrivals(ref, amount, sem):
        return pltpu.make_async_copy(ref.at[pl.ds(0, amount)], ref.at[pl.ds(0, amount)], sem)

    side = math.isqrt(chips) if math.isqrt(chips) ** 2 == chips else 1
    height = chips // side

    def hops(offset):
        return min(offset[0], height - offset[0]) + min(offset[1], side - offset[1])

    offsets = sorted(((dy, dx) for dy in range(height) for dx in range(side)), key=hops, reverse=True)
    farthest_first = [
        (hops(o) == 0, lax.rem(chip // side + o[0], height) * side + lax.rem(lax.rem(chip, side) + o[1], side))
        for o in offsets
    ]

    def scatter(part, seen, phase, first, end):
        for here, to in farthest_first:

            wanted = (to >= first) & (to < end)

            @pl.when(wanted & (core == 0) if here else wanted)
            def _():
                pltpu.make_async_remote_copy(
                    src_ref=part.at[to],
                    dst_ref=seen.at[me],
                    send_sem=reduce_send.at[2 * phase],
                    recv_sem=reduce_recv.at[2 * phase],
                    device_id={"dp": 2 * to + 1},
                    device_id_type=pl.DeviceIdType.MESH,
                ).start()

    def summed(part, seen, phase):
        seen[me] = part[chip]
        arrivals(seen, replicas - 1, reduce_recv.at[2 * phase]).wait()
        return jnp.sum(seen[...].astype(F32), axis=0)

    def spread(source, total, phase, arrival, to_section, to_self):
        for here, to in farthest_first:
            for end in range(1 if here and not to_self else 2):
                pltpu.make_async_remote_copy(
                    src_ref=source.at[chip],
                    dst_ref=total.at[chip],
                    send_sem=reduce_send.at[2 * phase + 1],
                    recv_sem=reduce_recv.at[arrival],
                    device_id={"section": to_section, "dp": 2 * to + end},
                    device_id_type=pl.DeviceIdType.MESH,
                ).start()

    def gathered(total, phase):
        @pl.when(owner)
        def _():
            arrivals(total, tiles - 1, reduce_recv.at[2 * phase + 1]).wait()

        @pl.when(jnp.logical_not(owner))
        def _():
            arrivals(total, tiles, reduce_recv.at[2 * phase + 1]).wait()

    def finish_sends(seen, phase):
        @pl.when(owner)
        def _():
            arrivals(seen, tiles - 1, reduce_send.at[2 * phase]).wait()
            arrivals(seen, replicas - 1, reduce_send.at[2 * phase + 1]).wait()

        @pl.when(jnp.logical_not(owner))
        def _():
            arrivals(seen, tiles, reduce_send.at[2 * phase]).wait()

    @pl.when(lifts)
    def _():
        for i in range(5):
            lift(i).wait_recv()
        lower_sums()


    @pl.when(jnp.logical_not(lifted))
    def _():
        add_block(slice(None))
        pack_some(p_part, p_packed, 0, tiles)
        scatter(p_packed, p_seen, 0, 0, tiles)

    @pl.when(lifts & owner)
    def _():
        lower_total[chip] = summed(lower_packed, lower_seen, 2).astype(BF16)
        spread(lower_total, p_total, 2, 1, section - 1, True)

    @pl.when(jnp.logical_not(lifted) & owner)
    def _():
        p_total[chip] = summed(p_packed, p_seen, 0).astype(BF16)
        spread(p_total, p_total, 0, 1, section, False)

    @pl.when(jnp.logical_not(lifted))
    def _():
        gathered(p_total, 0)

    @pl.when(lifted)
    def _():
        arrivals(p_total, tiles, reduce_recv.at[1]).wait()

    def unpacked(first, count):
        halves = [p_total[j] for j in range(first, first + count)]
        return jnp.concatenate([half for tile in halves for half in (tile[:8].astype(F32), tile[8:].astype(F32))], axis=1)

    p_value = unpacked(0, value_tiles)
    p_out = unpacked(value_tiles, out_tiles)
    p_all[:, :dw] = p_value
    p_all[:, dw:] = p_out
    p_value, p_out = p_value.astype(BF16), p_out.astype(BF16)
    q_out = small_mm(mm_nt(p_out, values[...]) * scale, grads[...]) + mm(p_out, err_out[...])
    for j in range(value_tiles):
        q_packed[out_tiles + j] = packed(q_out[:, 2 * LANES * j : 2 * LANES * (j + 1)])
    scatter(q_packed, q_seen, 1, out_tiles, tiles)
    q_value = small_mm(mm(p_value, normed_t[...]) * scale, value_grad[...]) + mm(p_value, err_value[...])
    for j in range(out_tiles):
        q_packed[j] = packed(q_value[:, 2 * LANES * j : 2 * LANES * (j + 1)])
    scatter(q_packed, q_seen, 1, 0, out_tiles)

    def factors():
        grams = [
            lax.dot_general(
                x, x, (((1,), (1,)), ((), ())), precision=lax.Precision.HIGHEST, preferred_element_type=F32
            )
            for x in (p_all[:, :dw], p_all[:, dw:])
        ]
        return [inverse_factor(gram) for gram in grams]

    def solved(pair, extra):
        for_value, for_out = extra
        lower = jnp.where(chip < out_tiles, for_value, for_out)
        return jnp.concatenate([apply_small(lower, pair[:8]), apply_small(lower, pair[8:])], axis=0)

    extra = factors()

    @pl.when(owner)
    def _():
        q_total[chip] = solved(summed(q_packed, q_seen, 1), extra).astype(BF16)
        spread(q_total, q_total, 1, 3, section, False)

    gathered(q_total, 1)
    for j in range(tiles):
        ref, place = (out_value, j) if j < out_tiles else (out_out, j - out_tiles)
        tile = q_total[j].astype(F32)
        ref[:, 2 * LANES * place : 2 * LANES * place + LANES] = tile[:8]
        ref[:, 2 * LANES * place + LANES : 2 * LANES * (place + 1)] = tile[8:]
    finish_sends(q_seen, 1)

    @pl.when(jnp.logical_not(lifted))
    def _():
        finish_sends(p_seen, 0)

    @pl.when(lifts)
    def _():
        @pl.when(owner)
        def _():
            arrivals(lower_seen, tiles - 1, reduce_send.at[4]).wait()
            arrivals(lower_seen, replicas, reduce_send.at[5]).wait()

        @pl.when(jnp.logical_not(owner))
        def _():
            arrivals(lower_seen, tiles, reduce_send.at[4]).wait()

    @pl.when(section > 0)
    def _():
        def sent(b):
            for c in range(pieces):
                hop(b, c).wait_send()

        each_block(sent)

    @pl.when(lifted)
    def _():
        for i in range(5):
            lift(i).wait_send()


def solution(mesh):
    sections, replicas = mesh.shape["section"], mesh.shape["dp"]

    def shards(
        acts, out_grad, tok_count, norm_gain, w_value, w_out, err_value, err_out, start_q_value, start_q_out
    ):
        rows, dw = out_grad.shape
        hv, rank = start_q_value.shape[1:]
        tiles = (dw + hv) // (2 * LANES)
        blocks = rows // 16
        cuts = tuple(cut * dw // CUTS[-1] for cut in CUTS)
        any_space = pl.BlockSpec(memory_space=pl.ANY)
        vmem = pl.BlockSpec(memory_space=pltpu.VMEM)
        q_value, q_out = pl.pallas_call(
            functools.partial(kernel, sections, replicas, blocks, cuts, GROUPS),
            out_shape=(pltpu.VMEM((rank, hv), F32), pltpu.VMEM((rank, dw), F32)),
            in_specs=[any_space] * 2 + [pl.BlockSpec(memory_space=pltpu.SMEM)] + [any_space] * 7,
            out_specs=(vmem, vmem),
            scratch_shapes=[
                pltpu.VMEM((rows, dw), BF16),
                pltpu.VMEM((rows, dw), BF16),
                pltpu.VMEM((1, dw), F32),
                pltpu.VMEM((dw, hv), BF16),
                pltpu.VMEM((hv, dw), BF16),
                pltpu.VMEM((dw, hv), BF16),
                pltpu.VMEM((hv, dw), BF16),
                pltpu.VMEM((rank, hv), F32),
                pltpu.VMEM((rank, dw), F32),
                pltpu.VMEM((hv, dw), BF16),
                pltpu.VMEM((dw, hv), BF16),
                pltpu.VMEM((rows, dw), F32),
                pltpu.VMEM((rows, LANES), F32),
                pltpu.VMEM((rows, dw), BF16),
                pltpu.VMEM((rows, hv), BF16),
                pltpu.VMEM((rows, hv), F32),
                pltpu.VMEM((rows, dw), BF16),
                pltpu.VMEM((rows, dw), BF16),
                pltpu.VMEM((rows, hv), BF16),
                pltpu.VMEM((rows, dw), F32),
                pltpu.VMEM((rank, dw + hv), F32),
                pltpu.VMEM((rank, dw + hv), F32),
                pltpu.VMEM((tiles, 2 * rank, LANES), BF16),
                pltpu.VMEM((tiles, 2 * rank, LANES), BF16),
                pltpu.VMEM((tiles, 2 * rank, LANES), BF16),
                pltpu.VMEM((tiles, 2 * rank, LANES), BF16),
                pltpu.VMEM((replicas, 2 * rank, LANES), BF16),
                pltpu.VMEM((replicas, 2 * rank, LANES), BF16),
                pltpu.SemaphoreType.DMA((9,)),
                pltpu.SemaphoreType.DMA((blocks * (len(cuts) - 1),)),
                pltpu.SemaphoreType.DMA((blocks * (len(cuts) - 1),)),
                pltpu.SemaphoreType.DMA((6,)),
                pltpu.SemaphoreType.DMA((6,)),
                pltpu.VMEM((rows, dw), BF16),
                pltpu.VMEM((rows, hv), BF16),
                pltpu.VMEM((rank, dw), F32),
                pltpu.VMEM((rank, dw), F32),
                pltpu.VMEM((rank, dw + hv), F32),
                pltpu.VMEM((tiles, 2 * rank, LANES), BF16),
                pltpu.VMEM((replicas, 2 * rank, LANES), BF16),
                pltpu.VMEM((tiles, 2 * rank, LANES), BF16),
                pltpu.VMEM((rank, dw), F32),
                pltpu.VMEM((dw, rows), BF16),
                pltpu.SemaphoreType.DMA((5,)),
                pltpu.SemaphoreType.DMA((5,)),
            ],
            compiler_params=pltpu.CompilerParams(
                collective_id=0, has_side_effects=True, vmem_limit_bytes=60 * 2**20
            ),
            cost_estimate=pl.CostEstimate(flops=1_700_000_000, bytes_accessed=12_000_000, transcendentals=0),
        )(
            acts[0],
            out_grad,
            tok_count,
            norm_gain,
            w_value[0],
            w_out[0],
            err_value[0],
            err_out[0],
            start_q_value[0].T,
            start_q_out[0].T,
        )
        return q_value.T[None], q_out.T[None]

    placed = (
        P("section", "dp", None),
        P("dp", None),
        P("dp"),
        P("section", None),
        P("section", None, None),
        P("section", None, None),
        P("section", "dp", None),
        P("section", "dp", None),
        P("section", None, None),
        P("section", None, None),
    )
    return jax.shard_map(
        shards,
        mesh=mesh,
        in_specs=placed,
        out_specs=(P("section", None, None), P("section", None, None)),
        check_vma=False,
    )
```
